128 devices in a mesh: gx: 16 (over x_hi, y, core), gy: 8 (over z, x_lo).
Axes of the slice: x: 4 (x_hi: 2, x_lo: 2; x = x_hi * 2 + x_lo), y: 4, z: 4, core: 2. Of those that a mesh axis runs over, the one named last changes fastest.
Arguments:
- te_init: float32 [768, 256, 128], P(('gx', 'gy')), may hold values from 0.5 to 3
- source: float32 [768, 256, 128], P(('gx', 'gy')), may hold values from 0.01 to 0.5
- velocities: float32 [3, 16, 8, 16384], P(None, 'gx', 'gy'), may hold values from -6 to 6
- noise: float32 [3, 16, 8, 16384], P(None, 'gx', 'gy'), may hold values from -6 to 6
- cell_index: int32 [16, 8, 16384], P('gx', 'gy'), may hold values from 0 to 1535
- cell_lane: int32 [16, 8, 16384], P('gx', 'gy'), may hold values from 0 to 127
- brick_atoms: int32 [16, 8], P('gx', 'gy'), may hold values from 2048 to 16384, as said below
Outputs:
- electron_temp: float32 [768, 256, 128], P(('gx', 'gy'))
- forces: float32 [3, 16, 8, 16384], P(None, 'gx', 'gy')
The draws below stay inside these ranges and needn't reach their ends.
Inputs may be any that keep to these rules, and one draw needn't show every extreme that they name: `cell_index`: cell columns are depth-major within the brick: d * 32 + y. `brick_atoms`: live atoms fill slots 0 to count - 1 of their brick; at least one brick is full.
All inputs are finite; a program needn't handle non-finite values.
Results may differ from the reference program's by a relative error of at most 0.00011.
Values sent between devices are 32-bit elements; how exact they have to be, the bound alone decides.
No kernel may reach another device: no remote copies, remote signals or barrier semaphores. Data moves between devices by JAX's collectives and lax.ppermute only.
A program may use at most 64 MiB of HBM per device.

```python
import math
import jax
import jax.numpy as jnp
from jax import lax

CX = 48
CY = 32
NZ = 128
A_DEV = 16384
STEPS = 8
BRICKS_X = 16
BRICKS_Y = 8
NX = 768
NY = 256
N_GX = 16
N_GY = 8


def draw_brick_atoms(key, part):
    key = jax.random.fold_in(key, 7)
    key_counts, key_chosen = jax.random.split(key)
    counts = jax.random.randint(key_counts, (BRICKS_X * BRICKS_Y,), A_DEV // 8, A_DEV + 1)
    chosen = jax.random.randint(key_chosen, (), 0, BRICKS_X * BRICKS_Y)
    merged = jnp.where(jnp.arange(BRICKS_X * BRICKS_Y) == chosen, A_DEV, counts)
    return merged.reshape(BRICKS_X, BRICKS_Y).astype(jnp.int32)


def place_ends(drawn, own_key, low, largest):
    extent = drawn.shape
    place = [jax.random.randint(jax.random.fold_in(own_key, axis), (), 0, extent[axis]) for axis in range(len(extent))]
    drawn = drawn.at[tuple(place)].set(low)
    longest = extent.index(max(extent))
    place[longest] = (place[longest] + 1) % extent[longest]
    return drawn.at[tuple(place)].set(largest)


def shard_levels(rng, extent, pieces, smallest, top_value):
    def one(position, parts):
        steps = jax.random.uniform(jax.random.fold_in(jax.random.fold_in(rng, 6), position), (parts,), jnp.float32, smallest / len(pieces), top_value / len(pieces))
        return jnp.repeat(jnp.exp(steps), extent[position] // parts).reshape((-1,) + (1,) * (len(extent) - position - 1))

    loudness = one(*pieces[0])
    for cut in pieces[1:]:
        loudness = loudness * one(*cut)
    return loudness


def normal_values(stream_key, dims, scale, reach, pieces=(), kind=jnp.bfloat16):
    drawn = jax.random.normal(stream_key, dims, jnp.float32) * scale
    if len(pieces) > 0:
        drawn = shard_levels(stream_key, dims, pieces, -0.22, 0.18) * drawn
    return jnp.clip(drawn, min=-reach, max=reach).astype(kind)


def setup_inputs(seed: int = 0) -> dict:
    key_of = jax.random.split(jax.random.key(seed), 8)
    return {
        "te_init": jnp.clip(0.5 + 2.5 * jax.random.uniform(key_of[0], (NX, NY, NZ), jnp.float32) ** shard_levels(key_of[0], (NX, NY, NZ), ((0, 128),), -0.2, 0.2), 0.5, 3.0),
        "source": jnp.clip(jnp.exp(math.log(0.5) - 3.912023 * jax.random.uniform(key_of[1], (NX, NY, NZ), jnp.float32) ** shard_levels(key_of[1], (NX, NY, NZ), ((0, 128),), -0.2, 0.2)), 0.01, 0.5),
        "velocities": normal_values(key_of[2], (3, BRICKS_X, BRICKS_Y, A_DEV), 1.0, 6.0, ((1, 16), (2, 8)), jnp.float32),
        "noise": normal_values(key_of[3], (3, BRICKS_X, BRICKS_Y, A_DEV), 1.0, 6.0, ((1, 16), (2, 8)), jnp.float32),
        "cell_index": place_ends(jax.random.randint(key_of[4], (BRICKS_X, BRICKS_Y, A_DEV), 0, CX * CY), jax.random.fold_in(key_of[4], 1), 0, (CX * CY) - 1).astype(jnp.int32),
        "cell_lane": place_ends(jax.random.randint(key_of[5], (BRICKS_X, BRICKS_Y, A_DEV), 0, NZ), jax.random.fold_in(key_of[5], 1), 0, NZ - 1).astype(jnp.int32),
        "brick_atoms": draw_brick_atoms(jax.random.fold_in(key_of[7], 71), 0),
    }


CONDUCTIVITY = 0.08
COUPLING = 0.1
FRICTION = 0.5

def advance(extended, tally, kinetic, heating, ghost_y):
    interior = slice(1, -1)
    lateral = interior if ghost_y else slice(None)
    centre = extended[interior, lateral]
    conduct_ext = CONDUCTIVITY * jnp.sqrt(1.0 + extended * extended)
    conduct = conduct_ext[interior, lateral]
    neighbours = [(extended[2:, lateral], conduct_ext[2:, lateral]), (extended[:-2, lateral], conduct_ext[:-2, lateral])]
    if ghost_y:
        neighbours += [(extended[interior, 2:], conduct_ext[interior, 2:]), (extended[interior, :-2], conduct_ext[interior, :-2])]
    else:
        neighbours += [(jnp.roll(centre, -1, 1), jnp.roll(conduct, -1, 1)), (jnp.roll(centre, 1, 1), jnp.roll(conduct, 1, 1))]
    neighbours += [(jnp.roll(centre, -1, 2), jnp.roll(conduct, -1, 2)), (jnp.roll(centre, 1, 2), jnp.roll(conduct, 1, 2))]
    flux_sum = jnp.zeros_like(centre)
    for beside, beside_conduct in neighbours:
        flux_sum = flux_sum + 2.0 * conduct * beside_conduct / (conduct + beside_conduct) * (beside - centre)
    capacity = 1.0 + centre * centre
    return (centre + (flux_sum + COUPLING * kinetic + heating) / capacity) / (1.0 + COUPLING * tally / capacity)

def reference(te_init, source, velocities, noise, cell_index, cell_lane, brick_atoms):
    brick_cells = CX * CY * NZ
    bricks = N_GX * N_GY
    slot_ids = jnp.arange(A_DEV, dtype=jnp.int32)
    living = (slot_ids[None, None, :] < brick_atoms[:, :, None]).astype(jnp.float32)
    kinetic_atom = lax.optimization_barrier(jnp.sum(velocities * velocities, axis=0)) / 3.0
    offsets = (jnp.arange(bricks, dtype=jnp.int32) * brick_cells).reshape(N_GX, N_GY, 1)
    local_ids = (cell_index * NZ + cell_lane).astype(jnp.int32)
    global_ids = (offsets + local_ids).reshape(-1).astype(jnp.int32)
    tally = jax.ops.segment_sum(living.reshape(-1), global_ids, num_segments=bricks * brick_cells)
    kinetic = jax.ops.segment_sum((living * kinetic_atom).reshape(-1), global_ids, num_segments=bricks * brick_cells)

    def to_grid(field):
        return field.reshape(N_GX, N_GY, CX, CY, NZ).transpose(0, 2, 1, 3, 4).reshape(NX, NY, NZ)
    tally = to_grid(tally)
    kinetic = to_grid(kinetic)
    electron = te_init
    for substep in range(STEPS):
        extended = jnp.pad(electron, ((1, 1), (0, 0), (0, 0)), mode='edge')
        electron = advance(extended, tally, kinetic, source, False)
    returned = electron.reshape(N_GX, CX, N_GY, CY, NZ).transpose(0, 2, 1, 3, 4).reshape(-1)
    te_atom = returned[global_ids].reshape(N_GX, N_GY, A_DEV)
    forces = -FRICTION * velocities + jnp.sqrt(2.0 * FRICTION * te_atom)[None] * noise
    forces = forces * living[None]
    return (electron, forces)
```

```python
import math

import jax
import jax.numpy as jnp
from jax import lax
from jax.experimental import pallas as pl
from jax.experimental.pallas import tpu as pltpu
from jax.sharding import PartitionSpec as P

CX = 48
CY = 32
NZ = 128
STEPS = 8

CONDUCTIVITY = 0.08
COUPLING = 0.1
FRICTION = 0.5

HALO = 4
ROWS = CY + 2 * HALO
LAYERS = CX + 2 * HALO


def split_bf16(value):
    high = lax.reduce_precision(value, 8, 7)
    return high.astype(jnp.bfloat16), (value - high).astype(jnp.bfloat16)


def widened(field, parts):
    layers = field.shape[0]
    blocks = field.reshape(layers, parts, CY, NZ).transpose(1, 0, 2, 3)
    after = jnp.roll(blocks, -1, 0)[:, :, :HALO]
    before = jnp.roll(blocks, 1, 0)[:, :, CY - HALO :]
    return jnp.concatenate([blocks, after, before], 2).reshape(parts * layers, ROWS, NZ)


def to_both_sides(head, tail, axis):
    count = lax.axis_size(axis)
    from_before = lax.ppermute(tail, axis, [(i, (i + 1) % count) for i in range(count)])
    from_after = lax.ppermute(head, axis, [((i + 1) % count, i) for i in range(count)])
    return from_before, from_after


def substeps_kernel(
    place, te, heat, load, te_lo, te_hi, hl_lo, hl_hi, out, u_all, heat_all, load_all
):
    deep = HALO - 1
    u_all[:HALO] = te_lo[...]
    u_all[pl.ds(HALO, CX)] = te[...]
    u_all[pl.ds(HALO + CX, HALO)] = te_hi[...]
    heat_all[pl.ds(1, deep)] = hl_lo[0]
    heat_all[pl.ds(HALO, CX)] = heat[...]
    heat_all[pl.ds(HALO + CX, deep)] = hl_hi[0]
    load_all[pl.ds(1, deep)] = hl_lo[1]
    load_all[pl.ds(HALO, CX)] = load[...]
    load_all[pl.ds(HALO + CX, deep)] = hl_hi[1]
    low_end = place[0]
    high_end = place[1]

    def flux(u, r, v, q):
        return (v - u) / (r + q)

    def one_step(step, first, count):
        def face(layer):
            closed = ((layer == HALO - 1) & (low_end == 1)) | (
                (layer == HALO + CX - 1) & (high_end == 1)
            )
            return jnp.where(closed, 0.0, 1.0)

        u0 = u_all[first - 1]
        r0 = lax.rsqrt(1.0 + u0 * u0)
        u1 = u_all[first]
        c1 = 1.0 + u1 * u1
        r1 = lax.rsqrt(c1)
        below = flux(u0, r0, u1, r1) * face(first - 1)

        def one_layer(i, carry):
            u, c, r, below = carry
            layer = first + i
            v = u_all[layer + 1]
            cv = 1.0 + v * v
            rv = lax.rsqrt(cv)
            above = flux(u, r, v, rv) * face(layer)
            side = flux(u, r, pltpu.roll(u, ROWS - 1, 0), pltpu.roll(r, ROWS - 1, 0))
            lane = flux(u, r, pltpu.roll(u, NZ - 1, 1), pltpu.roll(r, NZ - 1, 1))
            total = (above - below) + (side - pltpu.roll(side, 1, 0)) + (lane - pltpu.roll(lane, 1, 1))
            new = (u * c + (2.0 * CONDUCTIVITY) * total + heat_all[layer]) / (c + load_all[layer])
            u_all[layer] = new
            return v, cv, rv, above

        lax.fori_loop(0, count, one_layer, (u1, c1, r1, below), unroll=2)

    for step in range(HALO):
        one_step(step, step + 1, LAYERS - 2 - 2 * step)
    out[...] = u_all[pl.ds(HALO, CX)]


def substeps(place, te, heat, load, te_lo, te_hi, hl_lo, hl_hi):
    vmem = pl.BlockSpec(memory_space=pltpu.VMEM)
    return pl.pallas_call(
        substeps_kernel,
        out_shape=jax.ShapeDtypeStruct((CX, ROWS, NZ), jnp.float32),
        in_specs=[pl.BlockSpec(memory_space=pltpu.SMEM)] + [vmem] * 7,
        out_specs=vmem,
        scratch_shapes=[pltpu.VMEM((LAYERS, ROWS, NZ), jnp.float32)] * 3,
        compiler_params=pltpu.CompilerParams(vmem_limit_bytes=32 * 1024 * 1024),
        cost_estimate=pl.CostEstimate(flops=40_000_000, bytes_accessed=6_000_000, transcendentals=0),
        name="substeps",
    )(place, te, heat, load, te_lo, te_hi, hl_lo, hl_hi)


def one_hot(ids, count):
    return (ids[:, None] == lax.iota(jnp.int32, count)[None, :]).astype(jnp.bfloat16)


def bin_atoms(column, lane_ids, living, energy, block):
    blocks = column.shape[0] // block
    high, low = split_bf16(energy)
    total = jnp.zeros((CX * CY, 3 * NZ), jnp.float32)
    for b in range(blocks):
        part = slice(b * block, (b + 1) * block)
        lane_hot = one_hot(lane_ids[part], NZ)
        weighted = jnp.concatenate(
            [lane_hot * w[part].astype(jnp.bfloat16)[:, None] for w in (living, high, low)], 1
        )
        total = total + lax.dot_general(
            one_hot(column[part], CX * CY),
            weighted,
            (((0,), (0,)), ((), ())),
            preferred_element_type=jnp.float32,
        )
    return (
        total[:, :NZ].reshape(CX, CY, NZ),
        (total[:, NZ : 2 * NZ] + total[:, 2 * NZ :]).reshape(CX, CY, NZ),
    )


def read_cells(table, column, lane_ids, block):
    blocks = column.shape[0] // block
    pair = jnp.concatenate(split_bf16(table), 1)
    values = []
    for b in range(blocks):
        part = slice(b * block, (b + 1) * block)
        rows = jnp.dot(
            one_hot(column[part], CX * CY), pair, preferred_element_type=jnp.float32
        )
        hot = lane_ids[part][:, None] == lax.iota(jnp.int32, NZ)[None, :]
        values.append(jnp.sum(jnp.where(hot, rows[:, :NZ] + rows[:, NZ:], 0.0), axis=1))
    return jnp.concatenate(values)


def on_device(te_init, source, velocities, noise, cell_index, cell_lane, brick_atoms):
    slot_count = cell_index.shape[2]
    block = math.gcd(slot_count, 8192)
    parts = lax.axis_size("gy")
    te = lax.all_to_all(widened(te_init, parts), "gy", split_axis=0, concat_axis=0, tiled=True)
    source = lax.all_to_all(widened(source, parts), "gy", split_axis=0, concat_axis=0, tiled=True)

    column = cell_index[0, 0]
    lane_ids = cell_lane[0, 0]
    living = (lax.iota(jnp.int32, slot_count) < brick_atoms[0, 0]).astype(jnp.float32)
    moving = velocities[:, 0, 0]
    kinetic_atom = jnp.sum(moving * moving, axis=0) / 3.0
    tally, kinetic = bin_atoms(column, lane_ids, living, living * kinetic_atom, block)
    binned = COUPLING * jnp.stack([kinetic, tally])
    before, after = to_both_sides(binned[:, :, :HALO], binned[:, :, CY - HALO :], "gy")
    binned = jnp.concatenate([binned, after, before], 2)
    heat = source + binned[0]
    load = binned[1]

    position = lax.axis_index("gx")
    final = lax.axis_size("gx") - 1
    place = jnp.stack([position == 0, position == final]).astype(jnp.int32)
    near = HALO - 1
    head = jnp.concatenate([te[:HALO], heat[:near], load[:near]], 0)
    tail = jnp.concatenate([te[CX - HALO :], heat[CX - near :], load[CX - near :]], 0)
    lo, hi = to_both_sides(head, tail, "gx")
    hl_lo = lo[HALO:].reshape(2, near, ROWS, NZ)
    hl_hi = hi[HALO:].reshape(2, near, ROWS, NZ)
    te = substeps(place, te, heat, load, lo[:HALO], hi[:HALO], hl_lo, hl_hi)

    before, after = to_both_sides(te[:, :HALO], te[:, CY - HALO : CY], "gy")
    te = jnp.concatenate([te[:, :CY], after, before], 1)
    lo, hi = to_both_sides(te[:HALO], te[CX - HALO :], "gx")
    te = substeps(place, te, heat, load, lo, hi, hl_lo, hl_hi)
    te = te[:, :CY]

    electron = lax.all_to_all(te, "gy", split_axis=0, concat_axis=0, tiled=True)
    electron = electron.reshape(parts, CX // parts, CY, NZ).transpose(1, 0, 2, 3)
    electron = electron.reshape(CX // parts, parts * CY, NZ)
    te_atom = read_cells(te.reshape(CX * CY, NZ), column, lane_ids, block)
    forces = (
        -FRICTION * moving + jnp.sqrt(2.0 * FRICTION * te_atom)[None] * noise[:, 0, 0]
    ) * living[None]
    return (electron, forces[:, None, None, :])


def solution(mesh):
    return jax.shard_map(
        on_device,
        mesh=mesh,
        in_specs=(
            P(("gx", "gy"), None, None),
            P(("gx", "gy"), None, None),
            P(None, "gx", "gy", None),
            P(None, "gx", "gy", None),
            P("gx", "gy", None),
            P("gx", "gy", None),
            P("gx", "gy"),
        ),
        out_specs=(P(("gx", "gy"), None, None), P(None, "gx", "gy", None)),
        check_vma=False,
    )
```

```python
import functools

import jax
import jax.numpy as jnp
from jax import lax
from jax.experimental import pallas as pl
from jax.experimental.pallas import tpu as pltpu
from jax.sharding import PartitionSpec as P

CX = 48
CY = 32
NZ = 128
CONDUCTIVITY = 0.08
COUPLING = 0.1
FRICTION = 0.5

HALO = 4
NEAR = HALO - 1
ROWS = CY + 2 * HALO
COLS = CX * CY
GROUP = 6
BLOCK = 2048
MIB = 1024 * 1024

VMEM = pl.BlockSpec(memory_space=pltpu.VMEM)
SMEM = pl.BlockSpec(memory_space=pltpu.SMEM)


def params(mib):
    return pltpu.CompilerParams(vmem_limit_bytes=mib * MIB)


def f32(*shape):
    return jax.ShapeDtypeStruct(shape, jnp.float32)


def inverse(value):
    return 1.0 / value


def flux(u, r, v, q):
    return (v - u) * inverse(r + q)


def renewed(u, c, r, below, above, heat, load):
    rows = u.shape[0]
    side = flux(u, r, pltpu.roll(u, rows - 1, 0), pltpu.roll(r, rows - 1, 0))
    lane = flux(u, r, pltpu.roll(u, NZ - 1, 1), pltpu.roll(r, NZ - 1, 1))
    total = (above - below) + (side - pltpu.roll(side, 1, 0)) + (lane - pltpu.roll(lane, 1, 1))
    return (u * c + (2.0 * CONDUCTIVITY) * total + heat) * inverse(c + load)


def with_root(u):
    c = 1.0 + u * u
    return c, lax.rsqrt(c)


def interior_kernel(te, heat, load, out, first, second):
    def step(source, target, shift):
        below_u = source[0]
        _, below_r = with_root(below_u)
        u = source[1]
        c, r = with_root(u)

        def turn(i, carry):
            u, c, r, below = carry
            for g in range(GROUP):
                layer = i * GROUP + g
                v = source[layer + 2]
                cv, rv = with_root(v)
                above = flux(u, r, v, rv)
                target[layer + shift] = renewed(u, c, r, below, above, heat[layer], load[layer])
                u, c, r, below = v, cv, rv, above
            return u, c, r, below

        lax.fori_loop(0, CX // GROUP, turn, (u, c, r, flux(below_u, below_r, u, r)))

    first[pl.ds(1, CX)] = te[...]
    for buffer in (first, second):
        buffer[0] = te[0]
        buffer[CX + 1] = te[CX - 1]
    step(first, second, 1)
    step(second, first, 1)
    step(first, second, 1)
    step(second, out, 0)


def interior(te, heat, load):
    return pl.pallas_call(
        interior_kernel,
        out_shape=f32(CX, ROWS, NZ),
        in_specs=[VMEM] * 3,
        out_specs=VMEM,
        scratch_shapes=[pltpu.VMEM((CX + 2, ROWS, NZ), jnp.float32)] * 2,
        compiler_params=params(32),
        cost_estimate=pl.CostEstimate(flops=0, bytes_accessed=25_000_000, transcendentals=0),
        name="interior",
    )(te, heat, load)


def band_steps(us, heats, loads, closed_face, closed):
    for step in range(1, HALO + 1):
        us = list(us)
        roots = [with_root(u) for u in us]
        faces = []
        for i in range(len(us) - 1):
            face = flux(us[i], roots[i][1], us[i + 1], roots[i + 1][1])
            if i + step - 1 == closed_face:
                face = jnp.where(closed, 0.0, face)
            faces.append(face)
        us = [
            renewed(
                us[i],
                *roots[i],
                faces[i - 1],
                faces[i],
                heats[i + step - 2],
                loads[i + step - 2],
            )
            for i in range(1, len(us) - 1)
        ]
    return us


def bands_kernel(last, place, te, heat, load, te_lo, te_hi, lo, hi, inner, out, *faces):
    many = 2 * HALO
    near = HALO + NEAR
    low = band_steps(
        [te_lo[i] for i in range(HALO)] + [te[i] for i in range(many)],
        [lo[HALO + i] for i in range(NEAR)] + [heat[i] for i in range(near)],
        [lo[HALO + NEAR + i] for i in range(NEAR)] + [load[i] for i in range(near)],
        HALO - 1,
        place[0] == 1,
    )
    high = band_steps(
        [te[CX - many + i] for i in range(many)] + [te_hi[i] for i in range(HALO)],
        [heat[CX - near + i] for i in range(near)] + [hi[HALO + i] for i in range(NEAR)],
        [load[CX - near + i] for i in range(near)] + [hi[HALO + NEAR + i] for i in range(NEAR)],
        many - 1,
        place[1] == 1,
    )
    out[pl.ds(HALO, CX - many)] = inner[pl.ds(HALO, CX - many), :CY]
    for i in range(HALO):
        out[i] = low[i][:CY]
        out[CX - HALO + i] = high[i][:CY]
    if not last:
        head, tail = faces
        half = CX // 2
        head[:, :HALO] = out[:half, :HALO]
        head[:, HALO:] = out[half:, :HALO]
        tail[:, :HALO] = out[:half, CY - HALO :]
        tail[:, HALO:] = out[half:, CY - HALO :]


def bands(last, place, te, heat, load, te_lo, te_hi, lo, hi, inner):
    face = f32(CX // 2, 2 * HALO, NZ)
    shapes = [f32(CX, CY, NZ)] + ([] if last else [face, face])
    return pl.pallas_call(
        functools.partial(bands_kernel, last),
        out_shape=shapes,
        in_specs=[SMEM] + [VMEM] * 8,
        out_specs=[VMEM] * len(shapes),
        compiler_params=params(32),
        cost_estimate=pl.CostEstimate(flops=0, bytes_accessed=8_000_000, transcendentals=0),
        name="bands",
    )(place, te, heat, load, te_lo, te_hi, lo, hi, inner)


def first_kernel(parts, fields, load_in, kinetic, before, after, te, heat, load, head, tail):
    layers = CX // parts
    for j in range(parts):
        te[pl.ds(j * layers, layers)] = fields[pl.ds(2 * j * layers, layers)]
        span = pl.ds(j * layers, layers)
        source = pl.ds((2 * j + 1) * layers, layers)
        heat[span, :CY] = fields[source, :CY] + kinetic[span]
        heat[span, CY:] = fields[source, CY:] + jnp.concatenate(
            [after[span, HALO:], before[span, HALO:]], 1
        )
        load[span, :CY] = load_in[span]
        load[span, CY:] = jnp.concatenate([after[span, :HALO], before[span, :HALO]], 1)
    head[:HALO] = te[:HALO]
    tail[:HALO] = te[CX - HALO :]
    for place, field in ((HALO, heat), (HALO + NEAR, load)):
        head[pl.ds(place, NEAR)] = field[:NEAR]
        tail[pl.ds(place, NEAR)] = field[CX - NEAR :]


def first_brick(parts, fields, load, kinetic, before, after):
    whole = f32(CX, ROWS, NZ)
    edge = f32(HALO + 2 * NEAR, ROWS, NZ)
    return pl.pallas_call(
        functools.partial(first_kernel, parts),
        out_shape=[whole, whole, whole, edge, edge],
        in_specs=[VMEM] * 5,
        out_specs=[VMEM] * 5,
        compiler_params=params(32),
        cost_estimate=pl.CostEstimate(flops=0, bytes_accessed=4_000_000, transcendentals=0),
        name="first_brick",
    )(fields, load, kinetic, before, after)


def second_kernel(middle, before, after, te, head, tail):
    half = CX // 2
    te[:, :CY] = middle[...]
    te[:half, CY:] = jnp.concatenate([after[:, :HALO], before[:, :HALO]], 1)
    te[half:, CY:] = jnp.concatenate([after[:, HALO:], before[:, HALO:]], 1)
    head[...] = te[:HALO]
    tail[...] = te[CX - HALO :]


def second_brick(middle, before, after):
    edge = f32(HALO, ROWS, NZ)
    return pl.pallas_call(
        second_kernel,
        out_shape=[f32(CX, ROWS, NZ), edge, edge],
        in_specs=[VMEM] * 3,
        out_specs=[VMEM] * 3,
        compiler_params=params(32),
        cost_estimate=pl.CostEstimate(flops=0, bytes_accessed=4_000_000, transcendentals=0),
        name="second_brick",
    )(middle, before, after)


def column_hot(column):
    ids = lax.broadcasted_iota(jnp.int16, (COLS, column.shape[1]), 0)
    hot = ids == column.astype(jnp.int16)
    return jnp.where(hot, jnp.bfloat16(1), jnp.bfloat16(0))


def lane_mask(lane):
    return lax.broadcasted_iota(jnp.int32, (NZ, lane.shape[1]), 0) == lane


def living_of(count, block):
    slot = pl.program_id(0) * block + lax.broadcasted_iota(jnp.int32, (1, block), 1)
    return jnp.where(slot < count[0, 0], 1.0, 0.0)


def bin_kernel(block, count, column, lane, velocities, load, kinetic, head, tail, sums):
    @pl.when(pl.program_id(0) == 0)
    def _():
        sums[...] = jnp.zeros_like(sums)

    living = living_of(count, block)
    moving = velocities[...]
    energy = living * (moving[0] * moving[0] + moving[1] * moving[1] + moving[2] * moving[2]) / 3.0
    mask = lane_mask(lane[...])
    spread = jnp.where(mask, energy, 0.0)
    high = spread.astype(jnp.bfloat16)
    low = (spread - high.astype(jnp.float32)).astype(jnp.bfloat16)
    weighted = jnp.concatenate([jnp.where(mask, living, 0.0).astype(jnp.bfloat16), high, low], 0)
    term = lax.dot_general(
        weighted,
        column_hot(column[...]),
        (((1,), (1,)), ((), ())),
        preferred_element_type=jnp.float32,
    )
    sums[:NZ] += term[:NZ]
    sums[NZ:] += term[NZ : 2 * NZ] + term[2 * NZ :]

    @pl.when(pl.program_id(0) == pl.num_programs(0) - 1)
    def _():
        layers = NZ // CY
        for j in range(COLS // NZ):
            part = pl.ds(j * NZ, NZ)
            span = pl.ds(j * layers, layers)
            tally = sums[:NZ, part]
            heat = sums[NZ:, part]
            load[span] = (COUPLING * tally.T).reshape(layers, CY, NZ)
            kinetic[span] = (COUPLING * heat.T).reshape(layers, CY, NZ)
        head[:, :HALO] = load[:, :HALO]
        head[:, HALO:] = kinetic[:, :HALO]
        tail[:, :HALO] = load[:, CY - HALO :]
        tail[:, HALO:] = kinetic[:, CY - HALO :]


def blocks_of(shape, block):
    return pl.BlockSpec(shape + (block,), lambda i: (0,) * len(shape) + (i,))


def whole_of(*shape):
    return pl.BlockSpec(shape, lambda i: (0,) * len(shape))


def bin_atoms(count, column, lane, velocities):
    slots = column.shape[1]
    block = min(BLOCK, slots)
    brick = (CX, CY, NZ)
    face = (CX, 2 * HALO, NZ)
    return pl.pallas_call(
        functools.partial(bin_kernel, block),
        grid=(slots // block,),
        out_shape=[f32(*brick), f32(*brick), f32(*face), f32(*face)],
        in_specs=[SMEM, blocks_of((1,), block), blocks_of((1,), block), blocks_of((3, 1), block)],
        out_specs=[whole_of(*brick), whole_of(*brick), whole_of(*face), whole_of(*face)],
        scratch_shapes=[pltpu.VMEM((2 * NZ, COLS), jnp.float32)],
        compiler_params=params(48),
        cost_estimate=pl.CostEstimate(
            flops=6 * slots * COLS * NZ, bytes_accessed=4_000_000, transcendentals=0
        ),
        name="bin_atoms",
    )(count, column, lane, velocities)


def read_kernel(block, count, te, column, lane, velocities, noise, forces, pair):
    @pl.when(pl.program_id(0) == 0)
    def _():
        table = te[...].T
        high = table.astype(jnp.bfloat16)
        pair[:NZ] = high
        pair[NZ:] = (table - high.astype(jnp.float32)).astype(jnp.bfloat16)

    rows = jnp.dot(pair[...], column_hot(column[...]), preferred_element_type=jnp.float32)
    picked = jnp.where(lane_mask(lane[...]), rows[:NZ] + rows[NZ:], 0.0)
    te_atom = jnp.sum(picked, axis=0, keepdims=True)
    drive = jnp.sqrt(2.0 * FRICTION * te_atom)
    forces[...] = living_of(count, block) * (-FRICTION * velocities[...] + drive * noise[...])


def read_atoms(count, te, column, lane, velocities, noise):
    slots = column.shape[1]
    block = min(BLOCK, slots)
    return pl.pallas_call(
        functools.partial(read_kernel, block),
        grid=(slots // block,),
        out_shape=f32(3, 1, slots),
        in_specs=[
            SMEM,
            whole_of(COLS, NZ),
            blocks_of((1,), block),
            blocks_of((1,), block),
            blocks_of((3, 1), block),
            blocks_of((3, 1), block),
        ],
        out_specs=blocks_of((3, 1), block),
        scratch_shapes=[pltpu.VMEM((2 * NZ, COLS), jnp.bfloat16)],
        compiler_params=params(48),
        cost_estimate=pl.CostEstimate(
            flops=4 * slots * COLS * NZ, bytes_accessed=4_000_000, transcendentals=0
        ),
        name="read_atoms",
    )(count, te, column, lane, velocities, noise)


def widened(field, parts):
    layers = field.shape[0]
    blocks = field.reshape(layers, parts, CY, NZ).transpose(1, 0, 2, 3)
    after = jnp.roll(blocks, -1, 0)[:, :, :HALO]
    before = jnp.roll(blocks, 1, 0)[:, :, CY - HALO :]
    return jnp.concatenate([blocks, after, before], 2)


def to_both_sides(head, tail, axis):
    count = lax.axis_size(axis)
    from_before = lax.ppermute(tail, axis, [(i, (i + 1) % count) for i in range(count)])
    from_after = lax.ppermute(head, axis, [((i + 1) % count, i) for i in range(count)])
    return from_before, from_after


def exchanged(blocks):
    return lax.all_to_all(blocks, "gy", split_axis=0, concat_axis=0, tiled=True)


def on_device(te_init, source, velocities, noise, cell_index, cell_lane, brick_atoms):
    parts = lax.axis_size("gy")
    layers = te_init.shape[0]
    fields = jnp.concatenate([widened(te_init, parts), widened(source, parts)], 1)
    fields = exchanged(fields.reshape(2 * parts * layers, ROWS, NZ))

    column = cell_index[0]
    lane = cell_lane[0]
    moving = velocities[:, 0]
    load, kinetic, head, tail = bin_atoms(brick_atoms, column, lane, moving)
    before, after = to_both_sides(head, tail, "gy")

    position = lax.axis_index("gx")
    final = lax.axis_size("gx") - 1
    place = jnp.stack([position == 0, position == final]).astype(jnp.int32)
    te, heat, load, head, tail = first_brick(parts, fields, load, kinetic, before, after)
    lo, hi = to_both_sides(head, tail, "gx")
    inner = interior(te, heat, load)
    middle, head, tail = bands(False, place, te, heat, load, lo, hi, lo, hi, inner)

    before, after = to_both_sides(head, tail, "gy")
    te, head, tail = second_brick(middle, before, after)
    te_lo, te_hi = to_both_sides(head, tail, "gx")
    inner = interior(te, heat, load)
    (te,) = bands(True, place, te, heat, load, te_lo, te_hi, lo, hi, inner)

    electron = exchanged(te).reshape(parts, layers, CY, NZ).transpose(1, 0, 2, 3)
    electron = electron.reshape(layers, parts * CY, NZ)
    forces = read_atoms(brick_atoms, te.reshape(COLS, NZ), column, lane, moving, noise[:, 0])
    return (electron, forces[:, None])


def solution(mesh):
    return jax.shard_map(
        on_device,
        mesh=mesh,
        in_specs=(
            P(("gx", "gy"), None, None),
            P(("gx", "gy"), None, None),
            P(None, "gx", "gy", None),
            P(None, "gx", "gy", None),
            P("gx", "gy", None),
            P("gx", "gy", None),
            P("gx", "gy"),
        ),
        out_specs=(P(("gx", "gy"), None, None), P(None, "gx", "gy", None)),
        check_vma=False,
    )
```

```python
import functools

import jax
import jax.numpy as jnp
from jax import lax
from jax.experimental import pallas as pl
from jax.experimental.pallas import tpu as pltpu
from jax.sharding import PartitionSpec as P

CX = 48
CY = 32
NZ = 128
CONDUCTIVITY = 0.08
COUPLING = 0.1
FRICTION = 0.5

HALO = 4
NEAR = HALO - 1
ROWS = CY + 2 * HALO
COLS = CX * CY
GROUP = 6
BLOCK = 4096
MIB = 1024 * 1024

VMEM = pl.BlockSpec(memory_space=pltpu.VMEM)
SMEM = pl.BlockSpec(memory_space=pltpu.SMEM)
ANY = pl.BlockSpec(memory_space=pl.ANY)


def params(mib):
    return pltpu.CompilerParams(vmem_limit_bytes=mib * MIB)


def f32(*shape):
    return jax.ShapeDtypeStruct(shape, jnp.float32)


def inverse(value):
    return 1.0 / value


def flux(u, r, v, q):
    return (v - u) * inverse(r + q)


def renewed(u, c, r, below, above, heat, load):
    rows = u.shape[0]
    side = flux(u, r, pltpu.roll(u, rows - 1, 0), pltpu.roll(r, rows - 1, 0))
    lane = flux(u, r, pltpu.roll(u, NZ - 1, 1), pltpu.roll(r, NZ - 1, 1))
    total = (above - below) + (side - pltpu.roll(side, 1, 0)) + (lane - pltpu.roll(lane, 1, 1))
    return (u * c + (2.0 * CONDUCTIVITY) * total + heat) * inverse(c + load)


def with_root(u):
    c = 1.0 + u * u
    return c, lax.rsqrt(c)


def interior_steps(first, second, heat, load, out):
    def step(source, target, shift):
        below_u = source[0]
        _, below_r = with_root(below_u)
        u = source[1]
        c, r = with_root(u)

        def turn(i, carry):
            u, c, r, below = carry
            for g in range(GROUP):
                layer = i * GROUP + g
                v = source[layer + 2]
                cv, rv = with_root(v)
                above = flux(u, r, v, rv)
                target[layer + shift] = renewed(u, c, r, below, above, heat[layer], load[layer])
                u, c, r, below = v, cv, rv, above
            return u, c, r, below

        lax.fori_loop(0, CX // GROUP, turn, (u, c, r, flux(below_u, below_r, u, r)))

    for buffer in (first, second):
        buffer[0] = first[1]
        buffer[CX + 1] = first[CX]
    step(first, second, 1)
    step(second, first, 1)
    step(first, second, 1)
    step(second, out, 0)


def padded_brick():
    return pltpu.VMEM((CX + 2, ROWS, NZ), jnp.float32)


def second_interior_kernel(te, heat, load, out, first, second):
    first[pl.ds(1, CX)] = te[...]
    interior_steps(first, second, heat, load, out)


def second_interior(te, heat, load):
    return pl.pallas_call(
        second_interior_kernel,
        out_shape=f32(CX, ROWS, NZ),
        in_specs=[VMEM] * 3,
        out_specs=VMEM,
        scratch_shapes=[padded_brick()] * 2,
        compiler_params=params(32),
        cost_estimate=pl.CostEstimate(flops=0, bytes_accessed=25_000_000, transcendentals=0),
        name="interior",
    )(te, heat, load)


def first_interior_kernel(
    parts, own_head, own_tail, load_in, kinetic, before, after, fields, out, heat, load, *scratch
):
    first, second, source, sems = scratch
    layers = CX // parts
    fetches = []
    for j in range(parts):
        at = 2 * j * layers
        te_here = first.at[pl.ds(1 + j * layers, layers)]
        source_here = source.at[pl.ds(j * layers, layers)]
        for k, here in enumerate((te_here, source_here)):
            there = fields.at[pl.ds(at + k * layers, layers)]
            fetches.append(pltpu.make_async_copy(there, here, sems.at[2 * j + k]))
    for fetch in fetches:
        fetch.start()
    for i in range(parts):
        span = pl.ds(i * layers, layers)
        load[span] = side_by_side(own_head, load_in, own_tail, after, before, span, 0)
    for fetch in fetches:
        fetch.wait()
    for i in range(parts):
        span = pl.ds(i * layers, layers)
        heat[span] = source[span] + side_by_side(
            own_head, kinetic, own_tail, after, before, span, HALO
        )
    interior_steps(first, second, heat, load, out)


def side_by_side(own_head, inner, own_tail, after, before, span, row):
    rows = slice(row, row + HALO)
    return jnp.concatenate(
        [own_head[span, rows], inner[span], own_tail[span, rows], after[span, rows], before[span, rows]],
        1,
    )


def first_interior(parts, *arrays):
    whole = f32(CX, ROWS, NZ)
    return pl.pallas_call(
        functools.partial(first_interior_kernel, parts),
        out_shape=[whole] * 3,
        in_specs=[VMEM] * 6 + [ANY],
        out_specs=[VMEM] * 3,
        scratch_shapes=[padded_brick()] * 2
        + [pltpu.VMEM((CX, ROWS, NZ), jnp.float32)]
        + [pltpu.SemaphoreType.DMA((2 * parts,))],
        compiler_params=params(32),
        cost_estimate=pl.CostEstimate(flops=0, bytes_accessed=30_000_000, transcendentals=0),
        name="first_interior",
    )(*arrays)


def band_steps(us, heats, loads, closed_face, closed):
    for step in range(1, HALO + 1):
        us = list(us)
        roots = [with_root(u) for u in us]
        faces = []
        for i in range(len(us) - 1):
            face = flux(us[i], roots[i][1], us[i + 1], roots[i + 1][1])
            if i + step - 1 == closed_face:
                face = jnp.where(closed, 0.0, face)
            faces.append(face)
        us = [
            renewed(
                us[i],
                *roots[i],
                faces[i - 1],
                faces[i],
                heats[i + step - 2],
                loads[i + step - 2],
            )
            for i in range(1, len(us) - 1)
        ]
    return us


def bands_kernel(last, place, te, heat, load, te_lo, te_hi, lo, hi, inner, out, *faces):
    many = 2 * HALO
    near = HALO + NEAR
    low = band_steps(
        [te_lo[i] for i in range(HALO)] + [te[i] for i in range(many)],
        [lo[HALO + i] for i in range(NEAR)] + [heat[i] for i in range(near)],
        [lo[HALO + NEAR + i] for i in range(NEAR)] + [load[i] for i in range(near)],
        HALO - 1,
        place[0] == 1,
    )
    high = band_steps(
        [te[te.shape[0] - many + i] for i in range(many)] + [te_hi[i] for i in range(HALO)],
        [heat[CX - near + i] for i in range(near)] + [hi[HALO + i] for i in range(NEAR)],
        [load[CX - near + i] for i in range(near)] + [hi[HALO + NEAR + i] for i in range(NEAR)],
        many - 1,
        place[1] == 1,
    )
    out[pl.ds(HALO, CX - many)] = inner[pl.ds(HALO, CX - many), :CY]
    for i in range(HALO):
        out[i] = low[i][:CY]
        out[CX - HALO + i] = high[i][:CY]
    if not last:
        head, tail = faces
        half = CX // 2
        head[:, :HALO] = out[:half, :HALO]
        head[:, HALO:] = out[half:, :HALO]
        tail[:, :HALO] = out[:half, CY - HALO :]
        tail[:, HALO:] = out[half:, CY - HALO :]


def bands(last, place, te, heat, load, te_lo, te_hi, lo, hi, inner):
    face = f32(CX // 2, 2 * HALO, NZ)
    shapes = [f32(CX, CY, NZ)] + ([] if last else [face, face])
    return pl.pallas_call(
        functools.partial(bands_kernel, last),
        out_shape=shapes,
        in_specs=[SMEM] + [VMEM] * 8,
        out_specs=[VMEM] * len(shapes),
        compiler_params=params(32),
        cost_estimate=pl.CostEstimate(flops=0, bytes_accessed=8_000_000, transcendentals=0),
        name="bands",
    )(place, te, heat, load, te_lo, te_hi, lo, hi, inner)


def edges_kernel(parts, *refs):
    inside, (fields, ends, head, tail, here, source, sems) = refs[:6], refs[6:]
    layers = CX // parts
    many = 2 * HALO
    fetches = []

    def fetch(there, here):
        copy = pltpu.make_async_copy(there, here, sems.at[len(fetches)])
        copy.start()
        fetches.append(copy)

    for k, first in enumerate((0, CX - many)):
        layer = first
        while layer < first + many:
            part = layer // layers
            count = min(first + many, (part + 1) * layers) - layer
            there = fields.at[pl.ds(layer + part * layers, count)]
            fetch(there, here.at[pl.ds(k * many + layer - first, count)])
            layer += count
    for k, first in enumerate((0, CX - NEAR)):
        layer = first
        while layer < first + NEAR:
            part = layer // layers
            count = min(first + NEAR, (part + 1) * layers) - layer
            there = fields.at[pl.ds(layer + (part + 1) * layers, count)]
            fetch(there, source.at[k, pl.ds(layer - first, count)])
            layer += count
    for copy in fetches:
        copy.wait()
    ends[...] = here[...]
    for k, (target, at) in enumerate(((head, 0), (tail, 2 * many - HALO))):
        own_head, own_tail, load_in, kinetic, before, after = inside
        span = pl.ds((0, CX - NEAR)[k], NEAR)
        target[:HALO] = here[pl.ds(at, HALO)]
        target[pl.ds(HALO, NEAR)] = source[k] + side_by_side(
            own_head, kinetic, own_tail, after, before, span, HALO
        )
        target[pl.ds(HALO + NEAR, NEAR)] = side_by_side(
            own_head, load_in, own_tail, after, before, span, 0
        )


def edges(parts, *arrays):
    edge = f32(HALO + 2 * NEAR, ROWS, NZ)
    ends = (4 * HALO, ROWS, NZ)
    return pl.pallas_call(
        functools.partial(edges_kernel, parts),
        out_shape=[f32(*ends), edge, edge],
        in_specs=[VMEM] * 6 + [ANY],
        out_specs=[VMEM] * 3,
        scratch_shapes=[
            pltpu.VMEM(ends, jnp.float32),
            pltpu.VMEM((2, NEAR, ROWS, NZ), jnp.float32),
            pltpu.SemaphoreType.DMA((16,)),
        ],
        compiler_params=params(32),
        cost_estimate=pl.CostEstimate(flops=0, bytes_accessed=2_000_000, transcendentals=0),
        name="edges",
    )(*arrays)


def widen_kernel(parts, te, source, out, here, halo, in_sems, out_sems):
    layers = te.shape[0]
    fetches = [
        pltpu.make_async_copy(field, here.at[f], in_sems.at[f])
        for f, field in enumerate((te, source))
    ]
    for fetch in fetches:
        fetch.start()
    sends = []
    for f in range(2):
        fetches[f].wait()
        span = pl.ds(f * layers, layers)
        for j in range(parts):
            after = (j + 1) % parts * CY
            before = (j - 1) % parts * CY + CY - HALO
            halo[j, span] = jnp.concatenate(
                [here[f, :, pl.ds(after, HALO)], here[f, :, pl.ds(before, HALO)]], 1
            )
            own = here.at[f, :, pl.ds(j * CY, CY)]
            for k, (piece, rows) in enumerate(
                ((own, pl.ds(0, CY)), (halo.at[j, span], pl.ds(CY, 2 * HALO)))
            ):
                send = pltpu.make_async_copy(piece, out.at[j, span, rows], out_sems.at[f, j, k])
                send.start()
                sends.append(send)
    for send in sends:
        send.wait()


def widened(te, source, parts):
    layers = te.shape[0]
    return pl.pallas_call(
        functools.partial(widen_kernel, parts),
        out_shape=f32(parts, 2 * layers, ROWS, NZ),
        in_specs=[ANY] * 2,
        out_specs=ANY,
        scratch_shapes=[
            pltpu.VMEM((2,) + te.shape, jnp.float32),
            pltpu.VMEM((parts, 2 * layers, 2 * HALO, NZ), jnp.float32),
            pltpu.SemaphoreType.DMA((2,)),
            pltpu.SemaphoreType.DMA((2, parts, 2)),
        ],
        compiler_params=params(63),
        cost_estimate=pl.CostEstimate(flops=0, bytes_accessed=4_000_000, transcendentals=0),
        name="widen",
    )(te, source)


def second_kernel(middle, before, after, te, head, tail):
    half = CX // 2
    te[:, :CY] = middle[...]
    te[:half, CY:] = jnp.concatenate([after[:, :HALO], before[:, :HALO]], 1)
    te[half:, CY:] = jnp.concatenate([after[:, HALO:], before[:, HALO:]], 1)
    head[...] = te[:HALO]
    tail[...] = te[CX - HALO :]


def second_brick(middle, before, after):
    edge = f32(HALO, ROWS, NZ)
    return pl.pallas_call(
        second_kernel,
        out_shape=[f32(CX, ROWS, NZ), edge, edge],
        in_specs=[VMEM] * 3,
        out_specs=[VMEM] * 3,
        compiler_params=params(32),
        cost_estimate=pl.CostEstimate(flops=0, bytes_accessed=4_000_000, transcendentals=0),
        name="second_brick",
    )(middle, before, after)


INNER = CY - 2 * HALO


def column_hot(column, columns):
    ids = lax.broadcasted_iota(jnp.int16, (columns, column.shape[1]), 0)
    hot = ids == column.astype(jnp.int16)
    return jnp.where(hot, jnp.bfloat16(1), jnp.bfloat16(0))


def face_column(column):
    layer, row = column // CY, column % CY
    side = jnp.where(row < HALO, row, jnp.where(row >= CY - HALO, row - INNER, -1))
    return jnp.where(side < 0, -1, layer * 2 * HALO + side)


def inner_column(column):
    layer, row = column // CY, column % CY
    inside = (row >= HALO) & (row < CY - HALO)
    return jnp.where(inside, layer * INNER + row - HALO, -1)


def lane_mask(lane):
    return lax.broadcasted_iota(jnp.int32, (NZ, lane.shape[1]), 0) == lane


def living_of(count, block):
    slot = pl.program_id(0) * block + lax.broadcasted_iota(jnp.int32, (1, block), 1)
    return jnp.where(slot < count[0, 0], 1.0, 0.0)


def bin_kernel(block, faces, count, column, lane, velocities, first, second, sums):
    @pl.when(pl.program_id(0) == 0)
    def _():
        sums[...] = jnp.zeros_like(sums)

    living = living_of(count, block)
    moving = velocities[...]
    energy = living * (moving[0] * moving[0] + moving[1] * moving[1] + moving[2] * moving[2]) / 3.0
    lanes = lax.broadcasted_iota(jnp.int16, (NZ, block), 0)
    mask = lanes == lane[...].astype(jnp.int16)
    high = energy.astype(jnp.bfloat16)
    low = (energy - high.astype(jnp.float32)).astype(jnp.bfloat16)
    weighted = jnp.concatenate(
        [jnp.where(mask, w, jnp.bfloat16(0)) for w in (living.astype(jnp.bfloat16), high, low)], 0
    )
    columns = sums.shape[1]
    place = face_column(column[...]) if faces else inner_column(column[...])
    term = lax.dot_general(
        weighted,
        column_hot(place, columns),
        (((1,), (1,)), ((), ())),
        preferred_element_type=jnp.float32,
    )
    sums[:NZ] += term[:NZ]
    sums[NZ:] += term[NZ : 2 * NZ] + term[2 * NZ :]

    @pl.when(pl.program_id(0) == pl.num_programs(0) - 1)
    def _():
        rows = columns // CX
        layers = NZ // (2 * HALO)
        for layer in range(0, CX, layers):
            part = pl.ds(layer * rows, layers * rows)
            span = pl.ds(layer, layers)
            load = (COUPLING * sums[:NZ, part].T).reshape(layers, rows, NZ)
            kinetic = (COUPLING * sums[NZ:, part].T).reshape(layers, rows, NZ)
            if faces:
                for target, side in ((first, slice(0, HALO)), (second, slice(HALO, 2 * HALO))):
                    target[span, :HALO] = load[:, side]
                    target[span, HALO:] = kinetic[:, side]
            else:
                first[span] = load
                second[span] = kinetic


def blocks_of(shape, block):
    return pl.BlockSpec(shape + (block,), lambda i: (0,) * len(shape) + (i,))


def whole_of(*shape):
    return pl.BlockSpec(shape, lambda i: (0,) * len(shape))


def bin_atoms(faces, count, column, lane, velocities):
    slots = column.shape[1]
    block = min(BLOCK, slots)
    rows = 2 * HALO if faces else INNER
    result = (CX, rows, NZ)
    return pl.pallas_call(
        functools.partial(bin_kernel, block, faces),
        grid=(slots // block,),
        out_shape=[f32(*result)] * 2,
        in_specs=[SMEM, blocks_of((1,), block), blocks_of((1,), block), blocks_of((3, 1), block)],
        out_specs=[whole_of(*result)] * 2,
        scratch_shapes=[pltpu.VMEM((2 * NZ, CX * rows), jnp.float32)],
        compiler_params=params(63 if faces else 48),
        cost_estimate=pl.CostEstimate(
            flops=6 * slots * CX * rows * NZ, bytes_accessed=4_000_000, transcendentals=0
        ),
        name="bin_faces" if faces else "bin_inner",
    )(count, column, lane, velocities)


def read_kernel(block, count, te, column, lane, velocities, noise, forces, pair):
    @pl.when(pl.program_id(0) == 0)
    def _():
        table = te[...].T
        high = table.astype(jnp.bfloat16)
        pair[:NZ] = high
        pair[NZ:] = (table - high.astype(jnp.float32)).astype(jnp.bfloat16)

    rows = jnp.dot(pair[...], column_hot(column[...], COLS), preferred_element_type=jnp.float32)
    picked = jnp.where(lane_mask(lane[...]), rows[:NZ] + rows[NZ:], 0.0)
    te_atom = jnp.sum(picked, axis=0, keepdims=True)
    drive = jnp.sqrt(2.0 * FRICTION * te_atom)
    forces[...] = living_of(count, block) * (-FRICTION * velocities[...] + drive * noise[...])


def read_atoms(count, te, column, lane, velocities, noise):
    slots = column.shape[1]
    block = min(BLOCK, slots)
    return pl.pallas_call(
        functools.partial(read_kernel, block),
        grid=(slots // block,),
        out_shape=f32(3, 1, slots),
        in_specs=[
            SMEM,
            whole_of(COLS, NZ),
            blocks_of((1,), block),
            blocks_of((1,), block),
            blocks_of((3, 1), block),
            blocks_of((3, 1), block),
        ],
        out_specs=blocks_of((3, 1), block),
        scratch_shapes=[pltpu.VMEM((2 * NZ, COLS), jnp.bfloat16)],
        compiler_params=params(48),
        cost_estimate=pl.CostEstimate(
            flops=4 * slots * COLS * NZ, bytes_accessed=4_000_000, transcendentals=0
        ),
        name="read_atoms",
    )(count, te, column, lane, velocities, noise)


def to_both_sides(head, tail, axis):
    count = lax.axis_size(axis)
    from_before = lax.ppermute(tail, axis, [(i, (i + 1) % count) for i in range(count)])
    from_after = lax.ppermute(head, axis, [((i + 1) % count, i) for i in range(count)])
    return from_before, from_after


def exchanged(blocks):
    return lax.all_to_all(blocks, "gy", split_axis=0, concat_axis=0, tiled=True)


def on_device(te_init, source, velocities, noise, cell_index, cell_lane, brick_atoms):
    parts = lax.axis_size("gy")
    layers = te_init.shape[0]
    fields = widened(te_init, source, parts)
    fields = exchanged(fields.reshape(2 * parts * layers, ROWS, NZ))

    column = cell_index[0]
    lane = cell_lane[0]
    moving = velocities[:, 0]
    own_head, own_tail = bin_atoms(True, brick_atoms, column, lane, moving)
    before, after = to_both_sides(own_head, own_tail, "gy")
    load, kinetic = bin_atoms(False, brick_atoms, column, lane, moving)

    position = lax.axis_index("gx")
    final = lax.axis_size("gx") - 1
    place = jnp.stack([position == 0, position == final]).astype(jnp.int32)
    arrays = (own_head, own_tail, load, kinetic, before, after, fields)
    ends, head, tail = edges(parts, *arrays)
    lo, hi = to_both_sides(head, tail, "gx")
    inner, heat, load = first_interior(parts, *arrays)
    middle, head, tail = bands(False, place, ends, heat, load, lo, hi, lo, hi, inner)

    before, after = to_both_sides(head, tail, "gy")
    te, head, tail = second_brick(middle, before, after)
    te_lo, te_hi = to_both_sides(head, tail, "gx")
    inner = second_interior(te, heat, load)
    (te,) = bands(True, place, te, heat, load, te_lo, te_hi, lo, hi, inner)

    electron = exchanged(te).reshape(parts, layers, CY, NZ).transpose(1, 0, 2, 3)
    electron = electron.reshape(layers, parts * CY, NZ)
    forces = read_atoms(brick_atoms, te.reshape(COLS, NZ), column, lane, moving, noise[:, 0])
    return (electron, forces[:, None])


def solution(mesh):
    return jax.shard_map(
        on_device,
        mesh=mesh,
        in_specs=(
            P(("gx", "gy"), None, None),
            P(("gx", "gy"), None, None),
            P(None, "gx", "gy", None),
            P(None, "gx", "gy", None),
            P("gx", "gy", None),
            P("gx", "gy", None),
            P("gx", "gy"),
        ),
        out_specs=(P(("gx", "gy"), None, None), P(None, "gx", "gy", None)),
        check_vma=False,
    )
```

```python
import functools

import jax
import jax.numpy as jnp
from jax import lax
from jax.experimental import pallas as pl
from jax.experimental.pallas import tpu as pltpu
from jax.sharding import PartitionSpec as P

CX = 48
CY = 32
NZ = 128
CONDUCTIVITY = 0.08
COUPLING = 0.1
FRICTION = 0.5

HALO = 4
NEAR = HALO - 1
ROWS = CY + 2 * HALO
COLS = CX * CY
BLOCK = 4096
MIB = 1024 * 1024

VMEM = pl.BlockSpec(memory_space=pltpu.VMEM)
SMEM = pl.BlockSpec(memory_space=pltpu.SMEM)
ANY = pl.BlockSpec(memory_space=pl.ANY)


def params(mib):
    return pltpu.CompilerParams(vmem_limit_bytes=mib * MIB)


def f32(*shape):
    return jax.ShapeDtypeStruct(shape, jnp.float32)


def inverse(value):
    return 1.0 / value


def flux(u, r, v, q):
    return (v - u) * inverse(r + q)


def renewed(u, c, r, below, above, heat, load):
    rows = u.shape[0]
    side = flux(u, r, pltpu.roll(u, rows - 1, 0), pltpu.roll(r, rows - 1, 0))
    lane = flux(u, r, pltpu.roll(u, NZ - 1, 1), pltpu.roll(r, NZ - 1, 1))
    total = (above - below) + (side - pltpu.roll(side, 1, 0)) + (lane - pltpu.roll(lane, 1, 1))
    return (u * c + (2.0 * CONDUCTIVITY) * total + heat) * inverse(c + load)


def with_root(u):
    c = 1.0 + u * u
    return c, lax.rsqrt(c)


def interior_steps(first, second, heat, load, out):
    def step(source, target, shift, spoiled, group):
        below_u = source[spoiled]
        _, below_r = with_root(below_u)
        u = source[spoiled + 1]
        c, r = with_root(u)

        def turn(i, carry):
            u, c, r, below = carry
            for g in range(group):
                layer = i * group + (spoiled + g)
                v = source[layer + 2]
                cv, rv = with_root(v)
                above = flux(u, r, v, rv)
                target[layer + shift] = renewed(u, c, r, below, above, heat[layer], load[layer])
                u, c, r, below = v, cv, rv, above
            return u, c, r, below

        turns = (CX - 2 * spoiled) // group
        lax.fori_loop(0, turns, turn, (u, c, r, flux(below_u, below_r, u, r)))

    for buffer in (first, second):
        buffer[0] = first[1]
        buffer[CX + 1] = first[CX]
    step(first, second, 1, 0, 8)
    step(second, first, 1, 0, 8)
    step(first, second, 1, NEAR, 7)
    step(second, out, 0, HALO, 8)


def padded_brick():
    return pltpu.VMEM((CX + 2, ROWS, NZ), jnp.float32)


def second_interior_kernel(te, heat, load, out, first, second):
    first[pl.ds(1, CX)] = te[...]
    interior_steps(first, second, heat, load, out)


def second_interior(te, heat, load):
    return pl.pallas_call(
        second_interior_kernel,
        out_shape=f32(CX, ROWS, NZ),
        in_specs=[VMEM] * 3,
        out_specs=VMEM,
        scratch_shapes=[padded_brick()] * 2,
        compiler_params=params(32),
        cost_estimate=pl.CostEstimate(flops=0, bytes_accessed=25_000_000, transcendentals=0),
        name="interior",
    )(te, heat, load)


def first_interior_kernel(
    parts, own_head, own_tail, load_in, kinetic, before, after, fields, out, heat, load, *scratch
):
    first, second, source, sems = scratch
    layers = CX // parts
    fetches = []
    for j in range(parts):
        at = 2 * j * layers
        te_here = first.at[pl.ds(1 + j * layers, layers)]
        source_here = source.at[pl.ds(j * layers, layers)]
        for k, here in enumerate((te_here, source_here)):
            there = fields.at[pl.ds(at + k * layers, layers)]
            fetches.append(pltpu.make_async_copy(there, here, sems.at[2 * j + k]))
    for fetch in fetches:
        fetch.start()
    for i in range(parts):
        span = pl.ds(i * layers, layers)
        load[span] = side_by_side(own_head, load_in, own_tail, after, before, span, 0)
    for fetch in fetches:
        fetch.wait()
    for i in range(parts):
        span = pl.ds(i * layers, layers)
        heat[span] = source[span] + side_by_side(
            own_head, kinetic, own_tail, after, before, span, HALO
        )
    interior_steps(first, second, heat, load, out)


def side_by_side(own_head, inner, own_tail, after, before, span, row):
    rows = slice(row, row + HALO)
    return jnp.concatenate(
        [own_head[span, rows], inner[span], own_tail[span, rows], after[span, rows], before[span, rows]],
        1,
    )


def first_interior(parts, *arrays):
    whole = f32(CX, ROWS, NZ)
    return pl.pallas_call(
        functools.partial(first_interior_kernel, parts),
        out_shape=[whole] * 3,
        in_specs=[VMEM] * 6 + [ANY],
        out_specs=[VMEM] * 3,
        scratch_shapes=[padded_brick()] * 2
        + [pltpu.VMEM((CX, ROWS, NZ), jnp.float32)]
        + [pltpu.SemaphoreType.DMA((2 * parts,))],
        compiler_params=params(32),
        cost_estimate=pl.CostEstimate(flops=0, bytes_accessed=30_000_000, transcendentals=0),
        name="first_interior",
    )(*arrays)


def band_steps(us, heats, loads, closed_face, closed):
    for step in range(1, HALO + 1):
        us = list(us)
        roots = [with_root(u) for u in us]
        faces = []
        for i in range(len(us) - 1):
            face = flux(us[i], roots[i][1], us[i + 1], roots[i + 1][1])
            if i + step - 1 == closed_face:
                face = jnp.where(closed, 0.0, face)
            faces.append(face)
        us = [
            renewed(
                us[i],
                *roots[i],
                faces[i - 1],
                faces[i],
                heats[i + step - 2],
                loads[i + step - 2],
            )
            for i in range(1, len(us) - 1)
        ]
    return us


def bands_kernel(last, place, te, heat, load, te_lo, te_hi, lo, hi, inner, out, *faces):
    many = 2 * HALO
    near = HALO + NEAR
    low = band_steps(
        [te_lo[i] for i in range(HALO)] + [te[i] for i in range(many)],
        [lo[HALO + i] for i in range(NEAR)] + [heat[i] for i in range(near)],
        [lo[HALO + NEAR + i] for i in range(NEAR)] + [load[i] for i in range(near)],
        HALO - 1,
        place[0] == 1,
    )
    high = band_steps(
        [te[te.shape[0] - many + i] for i in range(many)] + [te_hi[i] for i in range(HALO)],
        [heat[CX - near + i] for i in range(near)] + [hi[HALO + i] for i in range(NEAR)],
        [load[CX - near + i] for i in range(near)] + [hi[HALO + NEAR + i] for i in range(NEAR)],
        many - 1,
        place[1] == 1,
    )
    out[pl.ds(HALO, CX - many)] = inner[pl.ds(HALO, CX - many), :CY]
    for i in range(HALO):
        out[i] = low[i][:CY]
        out[CX - HALO + i] = high[i][:CY]
    if not last:
        head, tail = faces
        half = CX // 2
        head[:, :HALO] = out[:half, :HALO]
        head[:, HALO:] = out[half:, :HALO]
        tail[:, :HALO] = out[:half, CY - HALO :]
        tail[:, HALO:] = out[half:, CY - HALO :]


def bands(last, place, te, heat, load, te_lo, te_hi, lo, hi, inner):
    face = f32(CX // 2, 2 * HALO, NZ)
    shapes = [f32(CX, CY, NZ)] + ([] if last else [face, face])
    return pl.pallas_call(
        functools.partial(bands_kernel, last),
        out_shape=shapes,
        in_specs=[SMEM] + [VMEM] * 8,
        out_specs=[VMEM] * len(shapes),
        compiler_params=params(32),
        cost_estimate=pl.CostEstimate(flops=0, bytes_accessed=8_000_000, transcendentals=0),
        name="bands",
    )(place, te, heat, load, te_lo, te_hi, lo, hi, inner)


def edges_kernel(parts, *refs):
    inside, (fields, ends, head, tail, here, source, sems) = refs[:6], refs[6:]
    layers = CX // parts
    many = 2 * HALO
    fetches = []

    def fetch(there, here):
        copy = pltpu.make_async_copy(there, here, sems.at[len(fetches)])
        copy.start()
        fetches.append(copy)

    for k, first in enumerate((0, CX - many)):
        layer = first
        while layer < first + many:
            part = layer // layers
            count = min(first + many, (part + 1) * layers) - layer
            there = fields.at[pl.ds(layer + part * layers, count)]
            fetch(there, here.at[pl.ds(k * many + layer - first, count)])
            layer += count
    for k, first in enumerate((0, CX - NEAR)):
        layer = first
        while layer < first + NEAR:
            part = layer // layers
            count = min(first + NEAR, (part + 1) * layers) - layer
            there = fields.at[pl.ds(layer + (part + 1) * layers, count)]
            fetch(there, source.at[k, pl.ds(layer - first, count)])
            layer += count
    for copy in fetches:
        copy.wait()
    ends[...] = here[...]
    for k, (target, at) in enumerate(((head, 0), (tail, 2 * many - HALO))):
        own_head, own_tail, load_in, kinetic, before, after = inside
        span = pl.ds((0, CX - NEAR)[k], NEAR)
        target[:HALO] = here[pl.ds(at, HALO)]
        target[pl.ds(HALO, NEAR)] = source[k] + side_by_side(
            own_head, kinetic, own_tail, after, before, span, HALO
        )
        target[pl.ds(HALO + NEAR, NEAR)] = side_by_side(
            own_head, load_in, own_tail, after, before, span, 0
        )


def edges(parts, *arrays):
    edge = f32(HALO + 2 * NEAR, ROWS, NZ)
    ends = (4 * HALO, ROWS, NZ)
    return pl.pallas_call(
        functools.partial(edges_kernel, parts),
        out_shape=[f32(*ends), edge, edge],
        in_specs=[VMEM] * 6 + [ANY],
        out_specs=[VMEM] * 3,
        scratch_shapes=[
            pltpu.VMEM(ends, jnp.float32),
            pltpu.VMEM((2, NEAR, ROWS, NZ), jnp.float32),
            pltpu.SemaphoreType.DMA((16,)),
        ],
        compiler_params=params(32),
        cost_estimate=pl.CostEstimate(flops=0, bytes_accessed=2_000_000, transcendentals=0),
        name="edges",
    )(*arrays)


def widen_kernel(parts, te, source, out, here, halo, in_sems, out_sems):
    layers = te.shape[0]
    fetches = [
        pltpu.make_async_copy(field, here.at[f], in_sems.at[f])
        for f, field in enumerate((te, source))
    ]
    for fetch in fetches:
        fetch.start()
    sends = []
    for f in range(2):
        fetches[f].wait()
        span = pl.ds(f * layers, layers)
        for j in range(parts):
            after = (j + 1) % parts * CY
            before = (j - 1) % parts * CY + CY - HALO
            halo[j, span] = jnp.concatenate(
                [here[f, :, pl.ds(after, HALO)], here[f, :, pl.ds(before, HALO)]], 1
            )
            own = here.at[f, :, pl.ds(j * CY, CY)]
            for k, (piece, rows) in enumerate(
                ((own, pl.ds(0, CY)), (halo.at[j, span], pl.ds(CY, 2 * HALO)))
            ):
                send = pltpu.make_async_copy(piece, out.at[j, span, rows], out_sems.at[f, j, k])
                send.start()
                sends.append(send)
    for send in sends:
        send.wait()


def widened(te, source, parts):
    layers = te.shape[0]
    return pl.pallas_call(
        functools.partial(widen_kernel, parts),
        out_shape=f32(parts, 2 * layers, ROWS, NZ),
        in_specs=[ANY] * 2,
        out_specs=ANY,
        scratch_shapes=[
            pltpu.VMEM((2,) + te.shape, jnp.float32),
            pltpu.VMEM((parts, 2 * layers, 2 * HALO, NZ), jnp.float32),
            pltpu.SemaphoreType.DMA((2,)),
            pltpu.SemaphoreType.DMA((2, parts, 2)),
        ],
        compiler_params=params(63),
        cost_estimate=pl.CostEstimate(flops=0, bytes_accessed=4_000_000, transcendentals=0),
        name="widen",
    )(te, source)


def second_kernel(middle, before, after, te, head, tail):
    half = CX // 2
    te[:, :CY] = middle[...]
    te[:half, CY:] = jnp.concatenate([after[:, :HALO], before[:, :HALO]], 1)
    te[half:, CY:] = jnp.concatenate([after[:, HALO:], before[:, HALO:]], 1)
    head[...] = te[:HALO]
    tail[...] = te[CX - HALO :]


def second_brick(middle, before, after):
    edge = f32(HALO, ROWS, NZ)
    return pl.pallas_call(
        second_kernel,
        out_shape=[f32(CX, ROWS, NZ), edge, edge],
        in_specs=[VMEM] * 3,
        out_specs=[VMEM] * 3,
        compiler_params=params(32),
        cost_estimate=pl.CostEstimate(flops=0, bytes_accessed=4_000_000, transcendentals=0),
        name="second_brick",
    )(middle, before, after)


INNER = CY - 2 * HALO


def column_hot(column, columns):
    ids = lax.broadcasted_iota(jnp.int16, (columns, column.shape[1]), 0)
    hot = ids == column.astype(jnp.int16)
    return jnp.where(hot, jnp.bfloat16(1), jnp.bfloat16(0))


def face_column(column):
    layer, row = column // CY, column % CY
    side = jnp.where(row < HALO, row, jnp.where(row >= CY - HALO, row - INNER, -1))
    return jnp.where(side < 0, -1, layer * 2 * HALO + side)


def inner_column(column):
    layer, row = column // CY, column % CY
    inside = (row >= HALO) & (row < CY - HALO)
    return jnp.where(inside, layer * INNER + row - HALO, -1)


def lane_mask(lane):
    return lax.broadcasted_iota(jnp.int32, (NZ, lane.shape[1]), 0) == lane


def living_of(count, block):
    slot = pl.program_id(0) * block + lax.broadcasted_iota(jnp.int32, (1, block), 1)
    return jnp.where(slot < count[0, 0], 1.0, 0.0)


def bin_kernel(block, faces, count, column, lane, velocities, first, second, sums):
    @pl.when(pl.program_id(0) == 0)
    def _():
        sums[...] = jnp.zeros_like(sums)

    living = living_of(count, block)
    moving = velocities[...]
    energy = living * (moving[0] * moving[0] + moving[1] * moving[1] + moving[2] * moving[2]) / 3.0
    lanes = lax.broadcasted_iota(jnp.int16, (NZ, block), 0)
    mask = lanes == lane[...].astype(jnp.int16)
    high = energy.astype(jnp.bfloat16)
    low = (energy - high.astype(jnp.float32)).astype(jnp.bfloat16)
    weighted = jnp.concatenate(
        [jnp.where(mask, w, jnp.bfloat16(0)) for w in (living.astype(jnp.bfloat16), high, low)], 0
    )
    columns = sums.shape[1]
    place = face_column(column[...]) if faces else inner_column(column[...])
    term = lax.dot_general(
        weighted,
        column_hot(place, columns),
        (((1,), (1,)), ((), ())),
        preferred_element_type=jnp.float32,
    )
    sums[:NZ] += term[:NZ]
    sums[NZ:] += term[NZ : 2 * NZ] + term[2 * NZ :]

    @pl.when(pl.program_id(0) == pl.num_programs(0) - 1)
    def _():
        rows = columns // CX
        layers = NZ // (2 * HALO)
        for layer in range(0, CX, layers):
            part = pl.ds(layer * rows, layers * rows)
            span = pl.ds(layer, layers)
            load = (COUPLING * sums[:NZ, part].T).reshape(layers, rows, NZ)
            kinetic = (COUPLING * sums[NZ:, part].T).reshape(layers, rows, NZ)
            if faces:
                for target, side in ((first, slice(0, HALO)), (second, slice(HALO, 2 * HALO))):
                    target[span, :HALO] = load[:, side]
                    target[span, HALO:] = kinetic[:, side]
            else:
                first[span] = load
                second[span] = kinetic


def blocks_of(shape, block):
    return pl.BlockSpec(shape + (block,), lambda i: (0,) * len(shape) + (i,))


def whole_of(*shape):
    return pl.BlockSpec(shape, lambda i: (0,) * len(shape))


def bin_atoms(faces, count, column, lane, velocities):
    slots = column.shape[1]
    block = min(BLOCK, slots)
    rows = 2 * HALO if faces else INNER
    result = (CX, rows, NZ)
    return pl.pallas_call(
        functools.partial(bin_kernel, block, faces),
        grid=(slots // block,),
        out_shape=[f32(*result)] * 2,
        in_specs=[SMEM, blocks_of((1,), block), blocks_of((1,), block), blocks_of((3, 1), block)],
        out_specs=[whole_of(*result)] * 2,
        scratch_shapes=[pltpu.VMEM((2 * NZ, CX * rows), jnp.float32)],
        compiler_params=params(63 if faces else 48),
        cost_estimate=pl.CostEstimate(
            flops=6 * slots * CX * rows * NZ, bytes_accessed=4_000_000, transcendentals=0
        ),
        name="bin_faces" if faces else "bin_inner",
    )(count, column, lane, velocities)


def read_kernel(block, count, te, column, lane, velocities, noise, forces, pair):
    @pl.when(pl.program_id(0) == 0)
    def _():
        rest = te[...].T * 8.0
        for k in range(3):
            piece = rest.astype(jnp.float8_e4m3fn)
            pair[k * NZ : (k + 1) * NZ] = piece
            rest = (rest - piece.astype(jnp.float32)) * 16.0

    hot = column_hot(column[...], COLS).astype(jnp.float8_e4m3fn)
    rows = jnp.dot(pair[...], hot, preferred_element_type=jnp.float32)
    value = rows[:NZ] * 0.125 + (rows[NZ : 2 * NZ] * (1 / 128) + rows[2 * NZ :] * (1 / 2048))
    picked = jnp.where(lane_mask(lane[...]), value, 0.0)
    te_atom = jnp.sum(picked, axis=0, keepdims=True)
    drive = jnp.sqrt(2.0 * FRICTION * te_atom)
    forces[...] = living_of(count, block) * (-FRICTION * velocities[...] + drive * noise[...])


def read_atoms(count, te, column, lane, velocities, noise):
    slots = column.shape[1]
    block = min(BLOCK, slots)
    return pl.pallas_call(
        functools.partial(read_kernel, block),
        grid=(slots // block,),
        out_shape=f32(3, 1, slots),
        in_specs=[
            SMEM,
            whole_of(COLS, NZ),
            blocks_of((1,), block),
            blocks_of((1,), block),
            blocks_of((3, 1), block),
            blocks_of((3, 1), block),
        ],
        out_specs=blocks_of((3, 1), block),
        scratch_shapes=[pltpu.VMEM((3 * NZ, COLS), jnp.float8_e4m3fn)],
        compiler_params=params(48),
        cost_estimate=pl.CostEstimate(
            flops=4 * slots * COLS * NZ, bytes_accessed=4_000_000, transcendentals=0
        ),
        name="read_atoms",
    )(count, te, column, lane, velocities, noise)


def to_both_sides(head, tail, axis):
    count = lax.axis_size(axis)
    from_before = lax.ppermute(tail, axis, [(i, (i + 1) % count) for i in range(count)])
    from_after = lax.ppermute(head, axis, [((i + 1) % count, i) for i in range(count)])
    return from_before, from_after


def exchanged(blocks):
    return lax.all_to_all(blocks, "gy", split_axis=0, concat_axis=0, tiled=True)


def on_device(te_init, source, velocities, noise, cell_index, cell_lane, brick_atoms):
    parts = lax.axis_size("gy")
    layers = te_init.shape[0]
    fields = widened(te_init, source, parts)
    fields = exchanged(fields.reshape(2 * parts * layers, ROWS, NZ))

    column = cell_index[0]
    lane = cell_lane[0]
    moving = velocities[:, 0]
    own_head, own_tail = bin_atoms(True, brick_atoms, column, lane, moving)
    before, after = to_both_sides(own_head, own_tail, "gy")
    load, kinetic = bin_atoms(False, brick_atoms, column, lane, moving)

    position = lax.axis_index("gx")
    final = lax.axis_size("gx") - 1
    place = jnp.stack([position == 0, position == final]).astype(jnp.int32)
    arrays = (own_head, own_tail, load, kinetic, before, after, fields)
    ends, head, tail = edges(parts, *arrays)
    lo, hi = to_both_sides(head, tail, "gx")
    inner, heat, load = first_interior(parts, *arrays)
    middle, head, tail = bands(False, place, ends, heat, load, lo, hi, lo, hi, inner)

    before, after = to_both_sides(head, tail, "gy")
    te, head, tail = second_brick(middle, before, after)
    te_lo, te_hi = to_both_sides(head, tail, "gx")
    inner = second_interior(te, heat, load)
    (te,) = bands(True, place, te, heat, load, te_lo, te_hi, lo, hi, inner)

    electron = exchanged(te).reshape(parts, layers, CY, NZ).transpose(1, 0, 2, 3)
    electron = electron.reshape(layers, parts * CY, NZ)
    forces = read_atoms(brick_atoms, te.reshape(COLS, NZ), column, lane, moving, noise[:, 0])
    return (electron, forces[:, None])


def solution(mesh):
    return jax.shard_map(
        on_device,
        mesh=mesh,
        in_specs=(
            P(("gx", "gy"), None, None),
            P(("gx", "gy"), None, None),
            P(None, "gx", "gy", None),
            P(None, "gx", "gy", None),
            P("gx", "gy", None),
            P("gx", "gy", None),
            P("gx", "gy"),
        ),
        out_specs=(P(("gx", "gy"), None, None), P(None, "gx", "gy", None)),
        check_vma=False,
    )
```

```python
import functools

import jax
import jax.numpy as jnp
from jax import lax
from jax.experimental import pallas as pl
from jax.experimental.pallas import tpu as pltpu
from jax.sharding import PartitionSpec as P

CX = 48
CY = 32
NZ = 128
CONDUCTIVITY = 0.08
COUPLING = 0.1
FRICTION = 0.5

HALO = 4
NEAR = HALO - 1
ROWS = CY + 2 * HALO
COLS = CX * CY
BLOCK = 4096
MIB = 1024 * 1024

VMEM = pl.BlockSpec(memory_space=pltpu.VMEM)
SMEM = pl.BlockSpec(memory_space=pltpu.SMEM)
ANY = pl.BlockSpec(memory_space=pl.ANY)


def params(mib):
    return pltpu.CompilerParams(vmem_limit_bytes=mib * MIB)


def f32(*shape):
    return jax.ShapeDtypeStruct(shape, jnp.float32)


def inverse(value):
    return 1.0 / value


def flux(u, r, v, q):
    return (v - u) * inverse(r + q)


def renewed(u, c, r, below, above, heat, load):
    rows = u.shape[0]
    side = flux(u, r, pltpu.roll(u, rows - 1, 0), pltpu.roll(r, rows - 1, 0))
    lane = flux(u, r, pltpu.roll(u, NZ - 1, 1), pltpu.roll(r, NZ - 1, 1))
    total = (above - below) + (side - pltpu.roll(side, 1, 0)) + (lane - pltpu.roll(lane, 1, 1))
    return (u * c + (2.0 * CONDUCTIVITY) * total + heat) * inverse(c + load)


def with_root(u):
    c = 1.0 + u * u
    return c, lax.rsqrt(c)


def interior_steps(first, second, heat, load, out):
    def step(source, target, shift, spoiled, group):
        below_u = source[spoiled]
        _, below_r = with_root(below_u)
        u = source[spoiled + 1]
        c, r = with_root(u)

        def turn(i, carry):
            u, c, r, below = carry
            for g in range(group):
                layer = i * group + (spoiled + g)
                v = source[layer + 2]
                cv, rv = with_root(v)
                above = flux(u, r, v, rv)
                target[layer + shift] = renewed(u, c, r, below, above, heat[layer], load[layer])
                u, c, r, below = v, cv, rv, above
            return u, c, r, below

        turns = (CX - 2 * spoiled) // group
        lax.fori_loop(0, turns, turn, (u, c, r, flux(below_u, below_r, u, r)))

    for buffer in (first, second):
        buffer[0] = first[1]
        buffer[CX + 1] = first[CX]
    step(first, second, 1, 0, 8)
    step(second, first, 1, 0, 8)
    step(first, second, 1, NEAR, 7)
    step(second, out, 0, HALO, 8)


def padded_brick():
    return pltpu.VMEM((CX + 2, ROWS, NZ), jnp.float32)


def second_interior_kernel(te, heat, load, out, first, second):
    first[pl.ds(1, CX)] = te[...]
    interior_steps(first, second, heat, load, out)


def second_interior(te, heat, load):
    return pl.pallas_call(
        second_interior_kernel,
        out_shape=f32(CX, ROWS, NZ),
        in_specs=[VMEM] * 3,
        out_specs=VMEM,
        scratch_shapes=[padded_brick()] * 2,
        compiler_params=params(32),
        cost_estimate=pl.CostEstimate(flops=0, bytes_accessed=25_000_000, transcendentals=0),
        name="interior",
    )(te, heat, load)


def first_interior_kernel(
    parts, own_head, own_tail, load_in, kinetic, halo, fields, out, heat, load, *scratch
):
    first, second, source, sems = scratch
    layers = CX // parts
    fetches = []
    for j in range(parts):
        at = 2 * j * layers
        te_here = first.at[pl.ds(1 + j * layers, layers)]
        source_here = source.at[pl.ds(j * layers, layers)]
        for k, here in enumerate((te_here, source_here)):
            there = fields.at[pl.ds(at + k * layers, layers)]
            fetches.append(pltpu.make_async_copy(there, here, sems.at[2 * j + k]))
    for fetch in fetches:
        fetch.start()
    for i in range(parts):
        span = pl.ds(i * layers, layers)
        load[span] = side_by_side(own_head, load_in, own_tail, halo, span, 0)
    for fetch in fetches:
        fetch.wait()
    for i in range(parts):
        span = pl.ds(i * layers, layers)
        heat[span] = source[span] + side_by_side(
            own_head, kinetic, own_tail, halo, span, 1
        )
    interior_steps(first, second, heat, load, out)


def side_by_side(own_head, inner, own_tail, halo, span, field):
    rows = slice(field * HALO, field * HALO + HALO)
    return jnp.concatenate(
        [own_head[span, rows], inner[span], own_tail[span, rows], halo[field, span]], 1
    )


def first_interior(parts, *arrays):
    whole = f32(CX, ROWS, NZ)
    return pl.pallas_call(
        functools.partial(first_interior_kernel, parts),
        out_shape=[whole] * 3,
        in_specs=[VMEM] * 5 + [ANY],
        out_specs=[VMEM] * 3,
        scratch_shapes=[padded_brick()] * 2
        + [pltpu.VMEM((CX, ROWS, NZ), jnp.float32)]
        + [pltpu.SemaphoreType.DMA((2 * parts,))],
        compiler_params=params(32),
        cost_estimate=pl.CostEstimate(flops=0, bytes_accessed=30_000_000, transcendentals=0),
        name="first_interior",
    )(*arrays)


def band_steps(us, heats, loads, closed_face, closed):
    for step in range(1, HALO + 1):
        us = list(us)
        roots = [with_root(u) for u in us]
        faces = []
        for i in range(len(us) - 1):
            face = flux(us[i], roots[i][1], us[i + 1], roots[i + 1][1])
            if i + step - 1 == closed_face:
                face = jnp.where(closed, 0.0, face)
            faces.append(face)
        us = [
            renewed(
                us[i],
                *roots[i],
                faces[i - 1],
                faces[i],
                heats[i + step - 2],
                loads[i + step - 2],
            )
            for i in range(1, len(us) - 1)
        ]
    return us


def bands_kernel(last, place, te, heat, load, te_lo, te_hi, lo, hi, inner, out, *faces):
    many = 2 * HALO
    near = HALO + NEAR
    low = band_steps(
        [te_lo[i] for i in range(HALO)] + [te[i] for i in range(many)],
        [lo[HALO + i] for i in range(NEAR)] + [heat[i] for i in range(near)],
        [lo[HALO + NEAR + i] for i in range(NEAR)] + [load[i] for i in range(near)],
        HALO - 1,
        place[0] == 1,
    )
    high = band_steps(
        [te[te.shape[0] - many + i] for i in range(many)] + [te_hi[i] for i in range(HALO)],
        [heat[CX - near + i] for i in range(near)] + [hi[HALO + i] for i in range(NEAR)],
        [load[CX - near + i] for i in range(near)] + [hi[HALO + NEAR + i] for i in range(NEAR)],
        many - 1,
        place[1] == 1,
    )
    out[pl.ds(HALO, CX - many)] = inner[pl.ds(HALO, CX - many), :CY]
    for i in range(HALO):
        out[i] = low[i][:CY]
        out[CX - HALO + i] = high[i][:CY]
    if not last:
        head, tail = faces
        half = CX // 2
        head[:, :HALO] = out[:half, :HALO]
        head[:, HALO:] = out[half:, :HALO]
        tail[:, :HALO] = out[:half, CY - HALO :]
        tail[:, HALO:] = out[half:, CY - HALO :]


def bands(last, place, te, heat, load, te_lo, te_hi, lo, hi, inner):
    face = f32(CX // 2, 2 * HALO, NZ)
    shapes = [f32(CX, CY, NZ)] + ([] if last else [face, face])
    return pl.pallas_call(
        functools.partial(bands_kernel, last),
        out_shape=shapes,
        in_specs=[SMEM] + [VMEM] * 8,
        out_specs=[VMEM] * len(shapes),
        compiler_params=params(32),
        cost_estimate=pl.CostEstimate(flops=0, bytes_accessed=8_000_000, transcendentals=0),
        name="bands",
    )(place, te, heat, load, te_lo, te_hi, lo, hi, inner)


def edges_kernel(parts, *refs):
    inside, (fields, ends, head, tail, halo, here, source, sems) = refs[:6], refs[6:]
    own_head, own_tail, load_in, kinetic, before, after = inside
    layers = CX // parts
    many = 2 * HALO
    fetches = []

    def fetch(there, here):
        copy = pltpu.make_async_copy(there, here, sems.at[len(fetches)])
        copy.start()
        fetches.append(copy)

    for k, first in enumerate((0, CX - many)):
        layer = first
        while layer < first + many:
            part = layer // layers
            count = min(first + many, (part + 1) * layers) - layer
            there = fields.at[pl.ds(layer + part * layers, count)]
            fetch(there, here.at[pl.ds(k * many + layer - first, count)])
            layer += count
    for k, first in enumerate((0, CX - NEAR)):
        layer = first
        while layer < first + NEAR:
            part = layer // layers
            count = min(first + NEAR, (part + 1) * layers) - layer
            there = fields.at[pl.ds(layer + (part + 1) * layers, count)]
            fetch(there, source.at[k, pl.ds(layer - first, count)])
            layer += count
    before, after = unpack(before), unpack(after)
    gap = jnp.zeros((CX, 2 * HALO - 2 * NEAR, NZ), jnp.float32)
    for field in range(2):
        rows = slice(field * NEAR, field * NEAR + NEAR)
        halo[field] = jnp.concatenate([after[:, rows], gap, before[:, rows]], 1)
    for copy in fetches:
        copy.wait()
    ends[...] = here[...]
    for k, (target, at) in enumerate(((head, 0), (tail, 2 * many - HALO))):
        span = pl.ds((0, CX - NEAR)[k], NEAR)
        target[:HALO] = here[pl.ds(at, HALO)]
        target[pl.ds(HALO, NEAR)] = source[k] + side_by_side(
            own_head, kinetic, own_tail, halo, span, 1
        )
        target[pl.ds(HALO + NEAR, NEAR)] = side_by_side(
            own_head, load_in, own_tail, halo, span, 0
        )


def edges(parts, *arrays):
    edge = f32(HALO + 2 * NEAR, ROWS, NZ)
    ends = (4 * HALO, ROWS, NZ)
    return pl.pallas_call(
        functools.partial(edges_kernel, parts),
        out_shape=[f32(*ends), edge, edge, f32(2, CX, 2 * HALO, NZ)],
        in_specs=[VMEM] * 6 + [ANY],
        out_specs=[VMEM] * 4,
        scratch_shapes=[
            pltpu.VMEM(ends, jnp.float32),
            pltpu.VMEM((2, NEAR, ROWS, NZ), jnp.float32),
            pltpu.SemaphoreType.DMA((16,)),
        ],
        compiler_params=params(32),
        cost_estimate=pl.CostEstimate(flops=0, bytes_accessed=2_000_000, transcendentals=0),
        name="edges",
    )(*arrays)


def widen_kernel(parts, te, source, out, here, halo, in_sems, out_sems):
    layers = te.shape[0]
    fetches = [
        pltpu.make_async_copy(field, here.at[f], in_sems.at[f])
        for f, field in enumerate((te, source))
    ]
    for fetch in fetches:
        fetch.start()
    sends = []
    for f in range(2):
        fetches[f].wait()
        span = pl.ds(f * layers, layers)
        for j in range(parts):
            after = (j + 1) % parts * CY
            before = (j - 1) % parts * CY + CY - HALO
            halo[j, span] = jnp.concatenate(
                [here[f, :, pl.ds(after, HALO)], here[f, :, pl.ds(before, HALO)]], 1
            )
            own = here.at[f, :, pl.ds(j * CY, CY)]
            for k, (piece, rows) in enumerate(
                ((own, pl.ds(0, CY)), (halo.at[j, span], pl.ds(CY, 2 * HALO)))
            ):
                send = pltpu.make_async_copy(piece, out.at[j, span, rows], out_sems.at[f, j, k])
                send.start()
                sends.append(send)
    for send in sends:
        send.wait()


def widened(te, source, parts):
    layers = te.shape[0]
    return pl.pallas_call(
        functools.partial(widen_kernel, parts),
        out_shape=f32(parts, 2 * layers, ROWS, NZ),
        in_specs=[ANY] * 2,
        out_specs=ANY,
        scratch_shapes=[
            pltpu.VMEM((2,) + te.shape, jnp.float32),
            pltpu.VMEM((parts, 2 * layers, 2 * HALO, NZ), jnp.float32),
            pltpu.SemaphoreType.DMA((2,)),
            pltpu.SemaphoreType.DMA((2, parts, 2)),
        ],
        compiler_params=params(63),
        cost_estimate=pl.CostEstimate(flops=0, bytes_accessed=4_000_000, transcendentals=0),
        name="widen",
    )(te, source)


def second_kernel(middle, before, after, te, head, tail):
    half = CX // 2
    te[:, :CY] = middle[...]
    te[:half, CY:] = jnp.concatenate([after[:, :HALO], before[:, :HALO]], 1)
    te[half:, CY:] = jnp.concatenate([after[:, HALO:], before[:, HALO:]], 1)
    head[...] = te[:HALO]
    tail[...] = te[CX - HALO :]


def second_brick(middle, before, after):
    edge = f32(HALO, ROWS, NZ)
    return pl.pallas_call(
        second_kernel,
        out_shape=[f32(CX, ROWS, NZ), edge, edge],
        in_specs=[VMEM] * 3,
        out_specs=[VMEM] * 3,
        compiler_params=params(32),
        cost_estimate=pl.CostEstimate(flops=0, bytes_accessed=4_000_000, transcendentals=0),
        name="second_brick",
    )(middle, before, after)


INNER = CY - 2 * HALO


def column_hot(column, columns):
    ids = lax.broadcasted_iota(jnp.int16, (columns, column.shape[1]), 0)
    hot = ids == column.astype(jnp.int16)
    return jnp.where(hot, jnp.bfloat16(1), jnp.bfloat16(0))


def face_column(column):
    layer, row = column // CY, column % CY
    side = jnp.where(row < HALO, row, jnp.where(row >= CY - HALO, row - INNER, -1))
    return jnp.where(side < 0, -1, layer * 2 * HALO + side)


def inner_column(column):
    layer, row = column // CY, column % CY
    inside = (row >= HALO) & (row < CY - HALO)
    return jnp.where(inside, layer * INNER + row - HALO, -1)


def lane_mask(lane):
    return lax.broadcasted_iota(jnp.int32, (NZ, lane.shape[1]), 0) == lane


def living_of(count, block):
    slot = pl.program_id(0) * block + lax.broadcasted_iota(jnp.int32, (1, block), 1)
    return jnp.where(slot < count[0, 0], 1.0, 0.0)


def bin_kernel(block, faces, count, column, lane, velocities, first, second, *rest):
    *sends, sums = rest

    @pl.when(pl.program_id(0) == 0)
    def _():
        sums[...] = jnp.zeros_like(sums)

    living = living_of(count, block)
    moving = velocities[...]
    energy = living * (moving[0] * moving[0] + moving[1] * moving[1] + moving[2] * moving[2]) / 3.0
    lanes = lax.broadcasted_iota(jnp.int16, (NZ, block), 0)
    mask = lanes == lane[...].astype(jnp.int16)
    high = energy.astype(jnp.bfloat16)
    low = (energy - high.astype(jnp.float32)).astype(jnp.bfloat16)
    weighted = jnp.concatenate(
        [jnp.where(mask, w, jnp.bfloat16(0)) for w in (living.astype(jnp.bfloat16), high, low)], 0
    )
    columns = sums.shape[1]
    place = face_column(column[...]) if faces else inner_column(column[...])
    term = lax.dot_general(
        weighted,
        column_hot(place, columns),
        (((1,), (1,)), ((), ())),
        preferred_element_type=jnp.float32,
    )
    sums[:NZ] += term[:NZ]
    sums[NZ:] += term[NZ : 2 * NZ] + term[2 * NZ :]

    @pl.when(pl.program_id(0) == pl.num_programs(0) - 1)
    def _():
        rows = columns // CX
        layers = NZ // (2 * HALO)
        for layer in range(0, CX, layers):
            part = pl.ds(layer * rows, layers * rows)
            span = pl.ds(layer, layers)
            load = (COUPLING * sums[:NZ, part].T).reshape(layers, rows, NZ)
            kinetic = (COUPLING * sums[NZ:, part].T).reshape(layers, rows, NZ)
            if faces:
                for target, side in ((first, slice(0, HALO)), (second, slice(HALO, 2 * HALO))):
                    target[span, :HALO] = load[:, side]
                    target[span, HALO:] = kinetic[:, side]
                for target, side in (
                    (sends[0], slice(0, NEAR)),
                    (sends[1], slice(2 * HALO - NEAR, 2 * HALO)),
                ):
                    pack(target, layer // 4, jnp.concatenate([load[:, side], kinetic[:, side]], 1))
            else:
                first[span] = load
                second[span] = kinetic


def pack(target, first, rows):
    fours = rows.reshape(rows.shape[0] // 4, 4, 2 * NEAR, NZ)
    span = pl.ds(first, fours.shape[0])
    for k in range(3):
        target[span, k] = jnp.concatenate([fours[:, k], fours[:, 3, 2 * k : 2 * k + 2]], 1)


def unpack(tiles):
    kept = [tiles[:, k] for k in range(3)]
    fourth = jnp.concatenate([tile[:, 2 * NEAR :] for tile in kept], 1)
    fours = jnp.stack([tile[:, : 2 * NEAR] for tile in kept] + [fourth], 1)
    return fours.reshape(4 * fours.shape[0], 2 * NEAR, NZ)


def blocks_of(shape, block):
    return pl.BlockSpec(shape + (block,), lambda i: (0,) * len(shape) + (i,))


def whole_of(*shape):
    return pl.BlockSpec(shape, lambda i: (0,) * len(shape))


def bin_atoms(faces, count, column, lane, velocities):
    slots = column.shape[1]
    block = min(BLOCK, slots)
    rows = 2 * HALO if faces else INNER
    result = (CX, rows, NZ)
    send = (CX // 4, 3, 2 * HALO, NZ)
    results = [result] * 2 + ([send] * 2 if faces else [])
    return pl.pallas_call(
        functools.partial(bin_kernel, block, faces),
        grid=(slots // block,),
        out_shape=[f32(*shape) for shape in results],
        in_specs=[SMEM, blocks_of((1,), block), blocks_of((1,), block), blocks_of((3, 1), block)],
        out_specs=[whole_of(*shape) for shape in results],
        scratch_shapes=[pltpu.VMEM((2 * NZ, CX * rows), jnp.float32)],
        compiler_params=params(63 if faces else 48),
        cost_estimate=pl.CostEstimate(
            flops=6 * slots * CX * rows * NZ, bytes_accessed=4_000_000, transcendentals=0
        ),
        name="bin_faces" if faces else "bin_inner",
    )(count, column, lane, velocities)


def read_kernel(block, count, te, column, lane, velocities, noise, forces, pair):
    @pl.when(pl.program_id(0) == 0)
    def _():
        rest = te[...].T * 8.0
        for k in range(3):
            piece = rest.astype(jnp.float8_e4m3fn)
            pair[k * NZ : (k + 1) * NZ] = piece
            rest = (rest - piece.astype(jnp.float32)) * 16.0

    hot = column_hot(column[...], COLS).astype(jnp.float8_e4m3fn)
    rows = jnp.dot(pair[...], hot, preferred_element_type=jnp.float32)
    value = rows[:NZ] * 0.125 + (rows[NZ : 2 * NZ] * (1 / 128) + rows[2 * NZ :] * (1 / 2048))
    picked = jnp.where(lane_mask(lane[...]), value, 0.0)
    te_atom = jnp.sum(picked, axis=0, keepdims=True)
    drive = jnp.sqrt(2.0 * FRICTION * te_atom)
    forces[...] = living_of(count, block) * (-FRICTION * velocities[...] + drive * noise[...])


def read_atoms(count, te, column, lane, velocities, noise):
    slots = column.shape[1]
    block = min(BLOCK, slots)
    return pl.pallas_call(
        functools.partial(read_kernel, block),
        grid=(slots // block,),
        out_shape=f32(3, 1, slots),
        in_specs=[
            SMEM,
            whole_of(COLS, NZ),
            blocks_of((1,), block),
            blocks_of((1,), block),
            blocks_of((3, 1), block),
            blocks_of((3, 1), block),
        ],
        out_specs=blocks_of((3, 1), block),
        scratch_shapes=[pltpu.VMEM((3 * NZ, COLS), jnp.float8_e4m3fn)],
        compiler_params=params(48),
        cost_estimate=pl.CostEstimate(
            flops=4 * slots * COLS * NZ, bytes_accessed=4_000_000, transcendentals=0
        ),
        name="read_atoms",
    )(count, te, column, lane, velocities, noise)


def to_both_sides(head, tail, axis):
    count = lax.axis_size(axis)
    from_before = lax.ppermute(tail, axis, [(i, (i + 1) % count) for i in range(count)])
    from_after = lax.ppermute(head, axis, [((i + 1) % count, i) for i in range(count)])
    return from_before, from_after


def exchanged(blocks):
    return lax.all_to_all(blocks, "gy", split_axis=0, concat_axis=0, tiled=True)


def on_device(te_init, source, velocities, noise, cell_index, cell_lane, brick_atoms):
    parts = lax.axis_size("gy")
    layers = te_init.shape[0]
    fields = widened(te_init, source, parts)
    fields = exchanged(fields.reshape(2 * parts * layers, ROWS, NZ))

    column = cell_index[0]
    lane = cell_lane[0]
    moving = velocities[:, 0]
    own_head, own_tail, head, tail = bin_atoms(True, brick_atoms, column, lane, moving)
    before, after = to_both_sides(head, tail, "gy")
    load, kinetic = bin_atoms(False, brick_atoms, column, lane, moving)

    position = lax.axis_index("gx")
    final = lax.axis_size("gx") - 1
    place = jnp.stack([position == 0, position == final]).astype(jnp.int32)
    ends, head, tail, halo = edges(
        parts, own_head, own_tail, load, kinetic, before, after, fields
    )
    lo, hi = to_both_sides(head, tail, "gx")
    inner, heat, load = first_interior(parts, own_head, own_tail, load, kinetic, halo, fields)
    middle, head, tail = bands(False, place, ends, heat, load, lo, hi, lo, hi, inner)

    before, after = to_both_sides(head, tail, "gy")
    te, head, tail = second_brick(middle, before, after)
    te_lo, te_hi = to_both_sides(head, tail, "gx")
    inner = second_interior(te, heat, load)
    (te,) = bands(True, place, te, heat, load, te_lo, te_hi, lo, hi, inner)

    electron = exchanged(te).reshape(parts, layers, CY, NZ).transpose(1, 0, 2, 3)
    electron = electron.reshape(layers, parts * CY, NZ)
    forces = read_atoms(brick_atoms, te.reshape(COLS, NZ), column, lane, moving, noise[:, 0])
    return (electron, forces[:, None])


def solution(mesh):
    return jax.shard_map(
        on_device,
        mesh=mesh,
        in_specs=(
            P(("gx", "gy"), None, None),
            P(("gx", "gy"), None, None),
            P(None, "gx", "gy", None),
            P(None, "gx", "gy", None),
            P("gx", "gy", None),
            P("gx", "gy", None),
            P("gx", "gy"),
        ),
        out_specs=(P(("gx", "gy"), None, None), P(None, "gx", "gy", None)),
        check_vma=False,
    )
```

```python
import functools

import jax
import jax.numpy as jnp
from jax import lax
from jax.experimental import pallas as pl
from jax.experimental.pallas import tpu as pltpu
from jax.sharding import PartitionSpec as P

CX = 48
CY = 32
NZ = 128
CONDUCTIVITY = 0.08
COUPLING = 0.1
FRICTION = 0.5

HALO = 4
NEAR = HALO - 1
ROWS = CY + 2 * HALO
COLS = CX * CY
BLOCK = 4096
FLOAT8 = jnp.float8_e4m3fn
MIB = 1024 * 1024

VMEM = pl.BlockSpec(memory_space=pltpu.VMEM)
SMEM = pl.BlockSpec(memory_space=pltpu.SMEM)
ANY = pl.BlockSpec(memory_space=pl.ANY)


def params(mib):
    return pltpu.CompilerParams(vmem_limit_bytes=mib * MIB)


def f32(*shape):
    return jax.ShapeDtypeStruct(shape, jnp.float32)


def inverse(value):
    return 1.0 / value


def flux(u, r, v, q):
    return (v - u) * inverse(r + q)


def renewed(u, c, r, below, above, heat, load):
    rows = u.shape[0]
    side = flux(u, r, pltpu.roll(u, rows - 1, 0), pltpu.roll(r, rows - 1, 0))
    lane = flux(u, r, pltpu.roll(u, NZ - 1, 1), pltpu.roll(r, NZ - 1, 1))
    total = (above - below) + (side - pltpu.roll(side, 1, 0)) + (lane - pltpu.roll(lane, 1, 1))
    return (u * c + (2.0 * CONDUCTIVITY) * total + heat) * inverse(c + load)


def with_root(u):
    c = 1.0 + u * u
    return c, lax.rsqrt(c)


def interior_steps(first, second, heat, load, out):
    def step(source, target, shift, spoiled, group):
        below_u = source[spoiled]
        _, below_r = with_root(below_u)
        u = source[spoiled + 1]
        c, r = with_root(u)

        def turn(i, carry):
            u, c, r, below = carry
            for g in range(group):
                layer = i * group + (spoiled + g)
                v = source[layer + 2]
                cv, rv = with_root(v)
                above = flux(u, r, v, rv)
                target[layer + shift] = renewed(u, c, r, below, above, heat[layer], load[layer])
                u, c, r, below = v, cv, rv, above
            return u, c, r, below

        turns = (CX - 2 * spoiled) // group
        lax.fori_loop(0, turns, turn, (u, c, r, flux(below_u, below_r, u, r)))

    for buffer in (first, second):
        buffer[0] = first[1]
        buffer[CX + 1] = first[CX]
    step(first, second, 1, 0, 8)
    step(second, first, 1, 0, 8)
    step(first, second, 1, NEAR, 7)
    step(second, out, 0, HALO, 8)


def padded_brick():
    return pltpu.VMEM((CX + 2, ROWS, NZ), jnp.float32)


def second_interior_kernel(te, heat, load, out, first, second):
    first[pl.ds(1, CX)] = te[...]
    interior_steps(first, second, heat, load, out)


def second_interior(te, heat, load):
    return pl.pallas_call(
        second_interior_kernel,
        out_shape=f32(CX, ROWS, NZ),
        in_specs=[VMEM] * 3,
        out_specs=VMEM,
        scratch_shapes=[padded_brick()] * 2,
        compiler_params=params(32),
        cost_estimate=pl.CostEstimate(flops=0, bytes_accessed=25_000_000, transcendentals=0),
        name="interior",
    )(te, heat, load)


def first_interior_kernel(
    parts, own_head, own_tail, load_in, kinetic, halo, fields, out, heat, load, *scratch
):
    first, second, source, sems = scratch
    layers = CX // parts
    fetches = []
    for j in range(parts):
        at = 2 * j * layers
        te_here = first.at[pl.ds(1 + j * layers, layers)]
        source_here = source.at[pl.ds(j * layers, layers)]
        for k, here in enumerate((te_here, source_here)):
            there = fields.at[pl.ds(at + k * layers, layers)]
            fetches.append(pltpu.make_async_copy(there, here, sems.at[2 * j + k]))
    for fetch in fetches:
        fetch.start()
    for i in range(parts):
        span = pl.ds(i * layers, layers)
        load[span] = side_by_side(own_head, load_in, own_tail, halo, span, 0)
    for fetch in fetches:
        fetch.wait()
    for i in range(parts):
        span = pl.ds(i * layers, layers)
        heat[span] = source[span] + side_by_side(
            own_head, kinetic, own_tail, halo, span, 1
        )
    interior_steps(first, second, heat, load, out)


def side_by_side(own_head, inner, own_tail, halo, span, field):
    rows = slice(field * HALO, field * HALO + HALO)
    return jnp.concatenate(
        [own_head[span, rows], inner[span], own_tail[span, rows], halo[field, span]], 1
    )


def first_interior(parts, *arrays):
    whole = f32(CX, ROWS, NZ)
    return pl.pallas_call(
        functools.partial(first_interior_kernel, parts),
        out_shape=[whole] * 3,
        in_specs=[VMEM] * 5 + [ANY],
        out_specs=[VMEM] * 3,
        scratch_shapes=[padded_brick()] * 2
        + [pltpu.VMEM((CX, ROWS, NZ), jnp.float32)]
        + [pltpu.SemaphoreType.DMA((2 * parts,))],
        compiler_params=params(32),
        cost_estimate=pl.CostEstimate(flops=0, bytes_accessed=30_000_000, transcendentals=0),
        name="first_interior",
    )(*arrays)


def band_steps(us, heats, loads, closed_face, closed):
    for step in range(1, HALO + 1):
        us = list(us)
        roots = [with_root(u) for u in us]
        faces = []
        for i in range(len(us) - 1):
            face = flux(us[i], roots[i][1], us[i + 1], roots[i + 1][1])
            if i + step - 1 == closed_face:
                face = jnp.where(closed, 0.0, face)
            faces.append(face)
        us = [
            renewed(
                us[i],
                *roots[i],
                faces[i - 1],
                faces[i],
                heats[i + step - 2],
                loads[i + step - 2],
            )
            for i in range(1, len(us) - 1)
        ]
    return us


def bands_kernel(last, place, te, heat, load, te_lo, te_hi, lo, hi, inner, out, *faces):
    many = 2 * HALO
    near = HALO + NEAR
    low = band_steps(
        [te_lo[i] for i in range(HALO)] + [te[i] for i in range(many)],
        [lo[HALO + i] for i in range(NEAR)] + [heat[i] for i in range(near)],
        [lo[HALO + NEAR + i] for i in range(NEAR)] + [load[i] for i in range(near)],
        HALO - 1,
        place[0] == 1,
    )
    high = band_steps(
        [te[te.shape[0] - many + i] for i in range(many)] + [te_hi[i] for i in range(HALO)],
        [heat[CX - near + i] for i in range(near)] + [hi[HALO + i] for i in range(NEAR)],
        [load[CX - near + i] for i in range(near)] + [hi[HALO + NEAR + i] for i in range(NEAR)],
        many - 1,
        place[1] == 1,
    )
    out[pl.ds(HALO, CX - many)] = inner[pl.ds(HALO, CX - many), :CY]
    for i in range(HALO):
        out[i] = low[i][:CY]
        out[CX - HALO + i] = high[i][:CY]
    if not last:
        head, tail = faces
        half = CX // 2
        head[:, :HALO] = out[:half, :HALO]
        head[:, HALO:] = out[half:, :HALO]
        tail[:, :HALO] = out[:half, CY - HALO :]
        tail[:, HALO:] = out[half:, CY - HALO :]


def bands(last, place, te, heat, load, te_lo, te_hi, lo, hi, inner):
    face = f32(CX // 2, 2 * HALO, NZ)
    shapes = [f32(CX, CY, NZ)] + ([] if last else [face, face])
    return pl.pallas_call(
        functools.partial(bands_kernel, last),
        out_shape=shapes,
        in_specs=[SMEM] + [VMEM] * 8,
        out_specs=[VMEM] * len(shapes),
        compiler_params=params(32),
        cost_estimate=pl.CostEstimate(flops=0, bytes_accessed=8_000_000, transcendentals=0),
        name="bands",
    )(place, te, heat, load, te_lo, te_hi, lo, hi, inner)


def edges_kernel(parts, *refs):
    inside, (fields, ends, head, tail, halo, here, source, sems) = refs[:6], refs[6:]
    own_head, own_tail, load_in, kinetic, before, after = inside
    layers = CX // parts
    many = 2 * HALO
    fetches = []

    def fetch(there, here):
        copy = pltpu.make_async_copy(there, here, sems.at[len(fetches)])
        copy.start()
        fetches.append(copy)

    for k, first in enumerate((0, CX - many)):
        layer = first
        while layer < first + many:
            part = layer // layers
            count = min(first + many, (part + 1) * layers) - layer
            there = fields.at[pl.ds(layer + part * layers, count)]
            fetch(there, here.at[pl.ds(k * many + layer - first, count)])
            layer += count
    for k, first in enumerate((0, CX - NEAR)):
        layer = first
        while layer < first + NEAR:
            part = layer // layers
            count = min(first + NEAR, (part + 1) * layers) - layer
            there = fields.at[pl.ds(layer + (part + 1) * layers, count)]
            fetch(there, source.at[k, pl.ds(layer - first, count)])
            layer += count
    before, after = unpack(before), unpack(after)
    gap = jnp.zeros((CX, 2 * HALO - 2 * NEAR, NZ), jnp.float32)
    for field in range(2):
        rows = slice(field * NEAR, field * NEAR + NEAR)
        halo[field] = jnp.concatenate([after[:, rows], gap, before[:, rows]], 1)
    for copy in fetches:
        copy.wait()
    ends[...] = here[...]
    for k, (target, at) in enumerate(((head, 0), (tail, 2 * many - HALO))):
        span = pl.ds((0, CX - NEAR)[k], NEAR)
        target[:HALO] = here[pl.ds(at, HALO)]
        target[pl.ds(HALO, NEAR)] = source[k] + side_by_side(
            own_head, kinetic, own_tail, halo, span, 1
        )
        target[pl.ds(HALO + NEAR, NEAR)] = side_by_side(
            own_head, load_in, own_tail, halo, span, 0
        )


def edges(parts, *arrays):
    edge = f32(HALO + 2 * NEAR, ROWS, NZ)
    ends = (4 * HALO, ROWS, NZ)
    return pl.pallas_call(
        functools.partial(edges_kernel, parts),
        out_shape=[f32(*ends), edge, edge, f32(2, CX, 2 * HALO, NZ)],
        in_specs=[VMEM] * 6 + [ANY],
        out_specs=[VMEM] * 4,
        scratch_shapes=[
            pltpu.VMEM(ends, jnp.float32),
            pltpu.VMEM((2, NEAR, ROWS, NZ), jnp.float32),
            pltpu.SemaphoreType.DMA((16,)),
        ],
        compiler_params=params(32),
        cost_estimate=pl.CostEstimate(flops=0, bytes_accessed=2_000_000, transcendentals=0),
        name="edges",
    )(*arrays)


def widen_kernel(parts, te, source, out, here, halo, in_sems, out_sems):
    layers = te.shape[0]
    fetches = [
        pltpu.make_async_copy(field, here.at[f], in_sems.at[f])
        for f, field in enumerate((te, source))
    ]
    for fetch in fetches:
        fetch.start()
    sends = []
    for f in range(2):
        fetches[f].wait()
        span = pl.ds(f * layers, layers)
        for j in range(parts):
            after = (j + 1) % parts * CY
            before = (j - 1) % parts * CY + CY - HALO
            halo[j, span] = jnp.concatenate(
                [here[f, :, pl.ds(after, HALO)], here[f, :, pl.ds(before, HALO)]], 1
            )
            own = here.at[f, :, pl.ds(j * CY, CY)]
            for k, (piece, rows) in enumerate(
                ((own, pl.ds(0, CY)), (halo.at[j, span], pl.ds(CY, 2 * HALO)))
            ):
                send = pltpu.make_async_copy(piece, out.at[j, span, rows], out_sems.at[f, j, k])
                send.start()
                sends.append(send)
    for send in sends:
        send.wait()


def widened(te, source, parts):
    layers = te.shape[0]
    return pl.pallas_call(
        functools.partial(widen_kernel, parts),
        out_shape=f32(parts, 2 * layers, ROWS, NZ),
        in_specs=[ANY] * 2,
        out_specs=ANY,
        scratch_shapes=[
            pltpu.VMEM((2,) + te.shape, jnp.float32),
            pltpu.VMEM((parts, 2 * layers, 2 * HALO, NZ), jnp.float32),
            pltpu.SemaphoreType.DMA((2,)),
            pltpu.SemaphoreType.DMA((2, parts, 2)),
        ],
        compiler_params=params(63),
        cost_estimate=pl.CostEstimate(flops=0, bytes_accessed=4_000_000, transcendentals=0),
        name="widen",
    )(te, source)


def second_kernel(middle, before, after, te, head, tail):
    half = CX // 2
    te[:, :CY] = middle[...]
    te[:half, CY:] = jnp.concatenate([after[:, :HALO], before[:, :HALO]], 1)
    te[half:, CY:] = jnp.concatenate([after[:, HALO:], before[:, HALO:]], 1)
    head[...] = te[:HALO]
    tail[...] = te[CX - HALO :]


def second_brick(middle, before, after):
    edge = f32(HALO, ROWS, NZ)
    return pl.pallas_call(
        second_kernel,
        out_shape=[f32(CX, ROWS, NZ), edge, edge],
        in_specs=[VMEM] * 3,
        out_specs=[VMEM] * 3,
        compiler_params=params(32),
        cost_estimate=pl.CostEstimate(flops=0, bytes_accessed=4_000_000, transcendentals=0),
        name="second_brick",
    )(middle, before, after)


INNER = CY - 2 * HALO


def column_hot(column, columns):
    ids = lax.broadcasted_iota(jnp.int16, (columns, column.shape[1]), 0)
    hot = ids == column.astype(jnp.int16)
    return jnp.where(hot, jnp.bfloat16(1), jnp.bfloat16(0))


def face_column(column):
    layer, row = column // CY, column % CY
    side = jnp.where(row < HALO, row, jnp.where(row >= CY - HALO, row - INNER, -1))
    return jnp.where(side < 0, -1, layer * 2 * HALO + side)


def inner_column(column):
    layer, row = column // CY, column % CY
    inside = (row >= HALO) & (row < CY - HALO)
    return jnp.where(inside, layer * INNER + row - HALO, -1)


def lane_mask(lane):
    return lax.broadcasted_iota(jnp.int32, (NZ, lane.shape[1]), 0) == lane


def living_of(count, block):
    slot = pl.program_id(0) * block + lax.broadcasted_iota(jnp.int32, (1, block), 1)
    return jnp.where(slot < count[0, 0], 1.0, 0.0)


def bin_kernel(block, faces, count, column, lane, velocities, first, second, *rest):
    *sends, sums = rest

    @pl.when(pl.program_id(0) == 0)
    def _():
        sums[...] = jnp.zeros_like(sums)

    living = living_of(count, block)
    moving = velocities[...]
    energy = living * (moving[0] * moving[0] + moving[1] * moving[1] + moving[2] * moving[2]) / 3.0
    mask = lane_mask(lane[...])
    rows = [jnp.where(mask, living, 0.0).astype(FLOAT8)]
    rest = jnp.where(mask, 8.0 * energy, 0.0)
    for _ in range(3):
        piece = rest.astype(FLOAT8)
        rows.append(piece)
        rest = 16.0 * (rest - piece.astype(jnp.float32))
    weighted = jnp.concatenate(rows, 0)
    columns = sums.shape[1]
    place = face_column(column[...]) if faces else inner_column(column[...])
    term = lax.dot_general(
        weighted,
        column_hot(place, columns).astype(FLOAT8),
        (((1,), (1,)), ((), ())),
        preferred_element_type=jnp.float32,
    )
    sums[:NZ] += term[:NZ]
    small = term[2 * NZ : 3 * NZ] * (1 / 128) + term[3 * NZ :] * (1 / 2048)
    sums[NZ:] += term[NZ : 2 * NZ] * 0.125 + small

    @pl.when(pl.program_id(0) == pl.num_programs(0) - 1)
    def _():
        rows = columns // CX
        layers = NZ // (2 * HALO)
        for layer in range(0, CX, layers):
            part = pl.ds(layer * rows, layers * rows)
            span = pl.ds(layer, layers)
            load = (COUPLING * sums[:NZ, part].T).reshape(layers, rows, NZ)
            kinetic = (COUPLING * sums[NZ:, part].T).reshape(layers, rows, NZ)
            if faces:
                for target, side in ((first, slice(0, HALO)), (second, slice(HALO, 2 * HALO))):
                    target[span, :HALO] = load[:, side]
                    target[span, HALO:] = kinetic[:, side]
                for target, side in (
                    (sends[0], slice(0, NEAR)),
                    (sends[1], slice(2 * HALO - NEAR, 2 * HALO)),
                ):
                    pack(target, layer // 4, jnp.concatenate([load[:, side], kinetic[:, side]], 1))
            else:
                first[span] = load
                second[span] = kinetic


def pack(target, first, rows):
    fours = rows.reshape(rows.shape[0] // 4, 4, 2 * NEAR, NZ)
    span = pl.ds(first, fours.shape[0])
    for k in range(3):
        target[span, k] = jnp.concatenate([fours[:, k], fours[:, 3, 2 * k : 2 * k + 2]], 1)


def unpack(tiles):
    kept = [tiles[:, k] for k in range(3)]
    fourth = jnp.concatenate([tile[:, 2 * NEAR :] for tile in kept], 1)
    fours = jnp.stack([tile[:, : 2 * NEAR] for tile in kept] + [fourth], 1)
    return fours.reshape(4 * fours.shape[0], 2 * NEAR, NZ)


def blocks_of(shape, block):
    return pl.BlockSpec(shape + (block,), lambda i: (0,) * len(shape) + (i,))


def whole_of(*shape):
    return pl.BlockSpec(shape, lambda i: (0,) * len(shape))


def bin_atoms(faces, count, column, lane, velocities):
    slots = column.shape[1]
    block = min(BLOCK, slots)
    rows = 2 * HALO if faces else INNER
    result = (CX, rows, NZ)
    send = (CX // 4, 3, 2 * HALO, NZ)
    results = [result] * 2 + ([send] * 2 if faces else [])
    return pl.pallas_call(
        functools.partial(bin_kernel, block, faces),
        grid=(slots // block,),
        out_shape=[f32(*shape) for shape in results],
        in_specs=[SMEM, blocks_of((1,), block), blocks_of((1,), block), blocks_of((3, 1), block)],
        out_specs=[whole_of(*shape) for shape in results],
        scratch_shapes=[pltpu.VMEM((2 * NZ, CX * rows), jnp.float32)],
        compiler_params=params(63 if faces else 48),
        cost_estimate=pl.CostEstimate(
            flops=6 * slots * CX * rows * NZ, bytes_accessed=4_000_000, transcendentals=0
        ),
        name="bin_faces" if faces else "bin_inner",
    )(count, column, lane, velocities)


def read_kernel(block, count, te, column, lane, velocities, noise, forces, pair):
    @pl.when(pl.program_id(0) == 0)
    def _():
        rest = te[...].T * 8.0
        for k in range(3):
            piece = rest.astype(FLOAT8)
            pair[k * NZ : (k + 1) * NZ] = piece
            rest = (rest - piece.astype(jnp.float32)) * 16.0

    hot = column_hot(column[...], COLS).astype(FLOAT8)
    rows = jnp.dot(pair[...], hot, preferred_element_type=jnp.float32)
    value = rows[:NZ] * 0.125 + (rows[NZ : 2 * NZ] * (1 / 128) + rows[2 * NZ :] * (1 / 2048))
    picked = jnp.where(lane_mask(lane[...]), value, 0.0)
    te_atom = jnp.sum(picked, axis=0, keepdims=True)
    drive = jnp.sqrt(2.0 * FRICTION * te_atom)
    forces[...] = living_of(count, block) * (-FRICTION * velocities[...] + drive * noise[...])


def read_atoms(count, te, column, lane, velocities, noise):
    slots = column.shape[1]
    block = min(BLOCK, slots)
    return pl.pallas_call(
        functools.partial(read_kernel, block),
        grid=(slots // block,),
        out_shape=f32(3, 1, slots),
        in_specs=[
            SMEM,
            whole_of(COLS, NZ),
            blocks_of((1,), block),
            blocks_of((1,), block),
            blocks_of((3, 1), block),
            blocks_of((3, 1), block),
        ],
        out_specs=blocks_of((3, 1), block),
        scratch_shapes=[pltpu.VMEM((3 * NZ, COLS), FLOAT8)],
        compiler_params=params(48),
        cost_estimate=pl.CostEstimate(
            flops=4 * slots * COLS * NZ, bytes_accessed=4_000_000, transcendentals=0
        ),
        name="read_atoms",
    )(count, te, column, lane, velocities, noise)


def to_both_sides(head, tail, axis):
    count = lax.axis_size(axis)
    from_before = lax.ppermute(tail, axis, [(i, (i + 1) % count) for i in range(count)])
    from_after = lax.ppermute(head, axis, [((i + 1) % count, i) for i in range(count)])
    return from_before, from_after


def exchanged(blocks):
    return lax.all_to_all(blocks, "gy", split_axis=0, concat_axis=0, tiled=True)


def on_device(te_init, source, velocities, noise, cell_index, cell_lane, brick_atoms):
    parts = lax.axis_size("gy")
    layers = te_init.shape[0]
    fields = widened(te_init, source, parts)
    fields = exchanged(fields.reshape(2 * parts * layers, ROWS, NZ))

    column = cell_index[0]
    lane = cell_lane[0]
    moving = velocities[:, 0]
    own_head, own_tail, head, tail = bin_atoms(True, brick_atoms, column, lane, moving)
    before, after = to_both_sides(head, tail, "gy")
    load, kinetic = bin_atoms(False, brick_atoms, column, lane, moving)

    position = lax.axis_index("gx")
    final = lax.axis_size("gx") - 1
    place = jnp.stack([position == 0, position == final]).astype(jnp.int32)
    ends, head, tail, halo = edges(
        parts, own_head, own_tail, load, kinetic, before, after, fields
    )
    lo, hi = to_both_sides(head, tail, "gx")
    inner, heat, load = first_interior(parts, own_head, own_tail, load, kinetic, halo, fields)
    middle, head, tail = bands(False, place, ends, heat, load, lo, hi, lo, hi, inner)

    before, after = to_both_sides(head, tail, "gy")
    te, head, tail = second_brick(middle, before, after)
    te_lo, te_hi = to_both_sides(head, tail, "gx")
    inner = second_interior(te, heat, load)
    (te,) = bands(True, place, te, heat, load, te_lo, te_hi, lo, hi, inner)

    electron = exchanged(te).reshape(parts, layers, CY, NZ).transpose(1, 0, 2, 3)
    electron = electron.reshape(layers, parts * CY, NZ)
    forces = read_atoms(brick_atoms, te.reshape(COLS, NZ), column, lane, moving, noise[:, 0])
    return (electron, forces[:, None])


def solution(mesh):
    return jax.shard_map(
        on_device,
        mesh=mesh,
        in_specs=(
            P(("gx", "gy"), None, None),
            P(("gx", "gy"), None, None),
            P(None, "gx", "gy", None),
            P(None, "gx", "gy", None),
            P("gx", "gy", None),
            P("gx", "gy", None),
            P("gx", "gy"),
        ),
        out_specs=(P(("gx", "gy"), None, None), P(None, "gx", "gy", None)),
        check_vma=False,
    )
```

```python
import functools

import jax
import jax.numpy as jnp
from jax import lax
from jax.experimental import pallas as pl
from jax.experimental.pallas import tpu as pltpu
from jax.sharding import PartitionSpec as P

CX = 48
CY = 32
NZ = 128
CONDUCTIVITY = 0.08
COUPLING = 0.1
FRICTION = 0.5

HALO = 4
NEAR = HALO - 1
ROWS = CY + 2 * HALO
COLS = CX * CY
BLOCK = 4096
FLOAT8 = jnp.float8_e4m3fn
MIB = 1024 * 1024

VMEM = pl.BlockSpec(memory_space=pltpu.VMEM)
SMEM = pl.BlockSpec(memory_space=pltpu.SMEM)
ANY = pl.BlockSpec(memory_space=pl.ANY)


def params(mib):
    return pltpu.CompilerParams(vmem_limit_bytes=mib * MIB)


def f32(*shape):
    return jax.ShapeDtypeStruct(shape, jnp.float32)


def inverse(value):
    return 1.0 / value


def flux(u, r, v, q):
    return (v - u) * inverse(r + q)


def renewed(u, c, r, below, above, heat, load):
    rows = u.shape[0]
    side = flux(u, r, pltpu.roll(u, rows - 1, 0), pltpu.roll(r, rows - 1, 0))
    lane = flux(u, r, pltpu.roll(u, NZ - 1, 1), pltpu.roll(r, NZ - 1, 1))
    total = (above - below) + (side - pltpu.roll(side, 1, 0)) + (lane - pltpu.roll(lane, 1, 1))
    return (u * c + (2.0 * CONDUCTIVITY) * total + heat) * inverse(c + load)


def with_root(u):
    c = 1.0 + u * u
    return c, lax.rsqrt(c)


def interior_steps(first, second, heat, load, out):
    def step(source, target, shift, spoiled, group):
        below_u = source[spoiled]
        _, below_r = with_root(below_u)
        u = source[spoiled + 1]
        c, r = with_root(u)

        def turn(i, carry):
            u, c, r, below = carry
            for g in range(group):
                layer = i * group + (spoiled + g)
                v = source[layer + 2]
                cv, rv = with_root(v)
                above = flux(u, r, v, rv)
                target[layer + shift] = renewed(u, c, r, below, above, heat[layer], load[layer])
                u, c, r, below = v, cv, rv, above
            return u, c, r, below

        turns = (CX - 2 * spoiled) // group
        lax.fori_loop(0, turns, turn, (u, c, r, flux(below_u, below_r, u, r)))

    for buffer in (first, second):
        buffer[0] = first[1]
        buffer[CX + 1] = first[CX]
    step(first, second, 1, 0, 8)
    step(second, first, 1, 0, 8)
    step(first, second, 1, NEAR, 7)
    step(second, out, 0, HALO, 8)


def padded_brick():
    return pltpu.VMEM((CX + 2, ROWS, NZ), jnp.float32)


def second_interior_kernel(te, heat, load, out, first, second):
    first[pl.ds(1, CX)] = te[...]
    interior_steps(first, second, heat, load, out)


def second_interior(te, heat, load):
    return pl.pallas_call(
        second_interior_kernel,
        out_shape=f32(CX, ROWS, NZ),
        in_specs=[VMEM] * 3,
        out_specs=VMEM,
        scratch_shapes=[padded_brick()] * 2,
        compiler_params=params(32),
        cost_estimate=pl.CostEstimate(flops=0, bytes_accessed=25_000_000, transcendentals=0),
        name="interior",
    )(te, heat, load)


def first_interior_kernel(
    own_head, own_tail, load_in, kinetic, halo, te, source, out, heat, load, first, second
):
    first[pl.ds(1, CX)] = te[...]
    for i in range(CX // 8):
        span = pl.ds(8 * i, 8)
        load[span] = side_by_side(own_head, load_in, own_tail, halo, span, 0)
        heat[span] = source[span] + side_by_side(own_head, kinetic, own_tail, halo, span, 1)
    interior_steps(first, second, heat, load, out)


def side_by_side(own_head, inner, own_tail, halo, span, field):
    rows = slice(field * HALO, field * HALO + HALO)
    return jnp.concatenate(
        [own_head[span, rows], inner[span], own_tail[span, rows], halo[field, span]], 1
    )


def first_interior(*arrays):
    whole = f32(CX, ROWS, NZ)
    return pl.pallas_call(
        first_interior_kernel,
        out_shape=[whole] * 3,
        in_specs=[VMEM] * 7,
        out_specs=[VMEM] * 3,
        scratch_shapes=[padded_brick()] * 2,
        compiler_params=params(32),
        cost_estimate=pl.CostEstimate(flops=0, bytes_accessed=30_000_000, transcendentals=0),
        name="first_interior",
    )(*arrays)


def band_steps(us, heats, loads, closed_face, closed):
    for step in range(1, HALO + 1):
        us = list(us)
        roots = [with_root(u) for u in us]
        faces = []
        for i in range(len(us) - 1):
            face = flux(us[i], roots[i][1], us[i + 1], roots[i + 1][1])
            if i + step - 1 == closed_face:
                face = jnp.where(closed, 0.0, face)
            faces.append(face)
        us = [
            renewed(
                us[i],
                *roots[i],
                faces[i - 1],
                faces[i],
                heats[i + step - 2],
                loads[i + step - 2],
            )
            for i in range(1, len(us) - 1)
        ]
    return us


def bands_kernel(last, place, te, heat, load, te_lo, te_hi, lo, hi, inner, out, *faces):
    many = 2 * HALO
    near = HALO + NEAR
    low = band_steps(
        [te_lo[i] for i in range(HALO)] + [te[i] for i in range(many)],
        [lo[HALO + i] for i in range(NEAR)] + [heat[i] for i in range(near)],
        [lo[HALO + NEAR + i] for i in range(NEAR)] + [load[i] for i in range(near)],
        HALO - 1,
        place[0] == 1,
    )
    high = band_steps(
        [te[te.shape[0] - many + i] for i in range(many)] + [te_hi[i] for i in range(HALO)],
        [heat[CX - near + i] for i in range(near)] + [hi[HALO + i] for i in range(NEAR)],
        [load[CX - near + i] for i in range(near)] + [hi[HALO + NEAR + i] for i in range(NEAR)],
        many - 1,
        place[1] == 1,
    )
    out[pl.ds(HALO, CX - many)] = inner[pl.ds(HALO, CX - many), :CY]
    for i in range(HALO):
        out[i] = low[i][:CY]
        out[CX - HALO + i] = high[i][:CY]
    if not last:
        head, tail = faces
        half = CX // 2
        head[:, :HALO] = out[:half, :HALO]
        head[:, HALO:] = out[half:, :HALO]
        tail[:, :HALO] = out[:half, CY - HALO :]
        tail[:, HALO:] = out[half:, CY - HALO :]


def bands(last, place, te, heat, load, te_lo, te_hi, lo, hi, inner):
    face = f32(CX // 2, 2 * HALO, NZ)
    shapes = [f32(CX, CY, NZ)] + ([] if last else [face, face])
    return pl.pallas_call(
        functools.partial(bands_kernel, last),
        out_shape=shapes,
        in_specs=[SMEM] + [VMEM] * 8,
        out_specs=[VMEM] * len(shapes),
        compiler_params=params(32),
        cost_estimate=pl.CostEstimate(flops=0, bytes_accessed=8_000_000, transcendentals=0),
        name="bands",
    )(place, te, heat, load, te_lo, te_hi, lo, hi, inner)


def unmix_kernel(parts, fields, te, source, sems):
    layers = CX // parts
    fetches = []
    for j in range(parts):
        for k, here in enumerate((te, source)):
            there = fields.at[pl.ds((2 * j + k) * layers, layers)]
            fetch = pltpu.make_async_copy(there, here.at[pl.ds(j * layers, layers)], sems.at[j, k])
            fetch.start()
            fetches.append(fetch)
    for fetch in fetches:
        fetch.wait()


def unmixed(parts, fields):
    return pl.pallas_call(
        functools.partial(unmix_kernel, parts),
        out_shape=[f32(CX, ROWS, NZ)] * 2,
        in_specs=[ANY],
        out_specs=[VMEM] * 2,
        scratch_shapes=[pltpu.SemaphoreType.DMA((parts, 2))],
        compiler_params=params(32),
        cost_estimate=pl.CostEstimate(flops=0, bytes_accessed=4_000_000, transcendentals=0),
        name="unmix",
    )(fields)


def edges_kernel(
    own_head, own_tail, load_in, kinetic, before, after, te, source, head, tail, halo
):
    before, after = unpack(before), unpack(after)
    gap = jnp.zeros((CX, 2 * HALO - 2 * NEAR, NZ), jnp.float32)
    for field in range(2):
        rows = slice(field * NEAR, field * NEAR + NEAR)
        halo[field] = jnp.concatenate([after[:, rows], gap, before[:, rows]], 1)
    for target, first, near in ((head, 0, 0), (tail, CX - HALO, CX - NEAR)):
        span = pl.ds(near, NEAR)
        target[:HALO] = te[pl.ds(first, HALO)]
        target[pl.ds(HALO, NEAR)] = source[span] + side_by_side(
            own_head, kinetic, own_tail, halo, span, 1
        )
        target[pl.ds(HALO + NEAR, NEAR)] = side_by_side(
            own_head, load_in, own_tail, halo, span, 0
        )


def edges(*arrays):
    edge = f32(HALO + 2 * NEAR, ROWS, NZ)
    return pl.pallas_call(
        edges_kernel,
        out_shape=[edge, edge, f32(2, CX, 2 * HALO, NZ)],
        in_specs=[VMEM] * 8,
        out_specs=[VMEM] * 3,
        compiler_params=params(32),
        cost_estimate=pl.CostEstimate(flops=0, bytes_accessed=2_000_000, transcendentals=0),
        name="edges",
    )(*arrays)


def widen_kernel(parts, te, source, out, here, halo, in_sems, out_sems):
    layers = te.shape[0]
    fetches = [
        pltpu.make_async_copy(field, here.at[f], in_sems.at[f])
        for f, field in enumerate((te, source))
    ]
    for fetch in fetches:
        fetch.start()
    sends = []
    for f in range(2):
        fetches[f].wait()
        span = pl.ds(f * layers, layers)
        for j in range(parts):
            after = (j + 1) % parts * CY
            before = (j - 1) % parts * CY + CY - HALO
            halo[j, span] = jnp.concatenate(
                [here[f, :, pl.ds(after, HALO)], here[f, :, pl.ds(before, HALO)]], 1
            )
            own = here.at[f, :, pl.ds(j * CY, CY)]
            for k, (piece, rows) in enumerate(
                ((own, pl.ds(0, CY)), (halo.at[j, span], pl.ds(CY, 2 * HALO)))
            ):
                send = pltpu.make_async_copy(piece, out.at[j, span, rows], out_sems.at[f, j, k])
                send.start()
                sends.append(send)
    for send in sends:
        send.wait()


def widened(te, source, parts):
    layers = te.shape[0]
    return pl.pallas_call(
        functools.partial(widen_kernel, parts),
        out_shape=f32(parts, 2 * layers, ROWS, NZ),
        in_specs=[ANY] * 2,
        out_specs=ANY,
        scratch_shapes=[
            pltpu.VMEM((2,) + te.shape, jnp.float32),
            pltpu.VMEM((parts, 2 * layers, 2 * HALO, NZ), jnp.float32),
            pltpu.SemaphoreType.DMA((2,)),
            pltpu.SemaphoreType.DMA((2, parts, 2)),
        ],
        compiler_params=params(63),
        cost_estimate=pl.CostEstimate(flops=0, bytes_accessed=4_000_000, transcendentals=0),
        name="widen",
    )(te, source)


def second_kernel(middle, before, after, te, head, tail):
    half = CX // 2
    te[:, :CY] = middle[...]
    te[:half, CY:] = jnp.concatenate([after[:, :HALO], before[:, :HALO]], 1)
    te[half:, CY:] = jnp.concatenate([after[:, HALO:], before[:, HALO:]], 1)
    head[...] = te[:HALO]
    tail[...] = te[CX - HALO :]


def second_brick(middle, before, after):
    edge = f32(HALO, ROWS, NZ)
    return pl.pallas_call(
        second_kernel,
        out_shape=[f32(CX, ROWS, NZ), edge, edge],
        in_specs=[VMEM] * 3,
        out_specs=[VMEM] * 3,
        compiler_params=params(32),
        cost_estimate=pl.CostEstimate(flops=0, bytes_accessed=4_000_000, transcendentals=0),
        name="second_brick",
    )(middle, before, after)


INNER = CY - 2 * HALO


def column_hot(column, columns):
    ids = lax.broadcasted_iota(jnp.int16, (columns, column.shape[1]), 0)
    hot = ids == column.astype(jnp.int16)
    return jnp.where(hot, jnp.bfloat16(1), jnp.bfloat16(0))


def face_column(column):
    layer, row = column // CY, column % CY
    side = jnp.where(row < HALO, row, jnp.where(row >= CY - HALO, row - INNER, -1))
    return jnp.where(side < 0, -1, layer * 2 * HALO + side)


def inner_column(column):
    layer, row = column // CY, column % CY
    inside = (row >= HALO) & (row < CY - HALO)
    return jnp.where(inside, layer * INNER + row - HALO, -1)


def lane_mask(lane):
    return lax.broadcasted_iota(jnp.int32, (NZ, lane.shape[1]), 0) == lane


def living_of(count, block):
    slot = pl.program_id(0) * block + lax.broadcasted_iota(jnp.int32, (1, block), 1)
    return jnp.where(slot < count[0, 0], 1.0, 0.0)


def bin_kernel(block, faces, count, column, lane, velocities, first, second, *rest):
    *sends, sums = rest

    @pl.when(pl.program_id(0) == 0)
    def _():
        sums[...] = jnp.zeros_like(sums)

    living = living_of(count, block)
    moving = velocities[...]
    energy = living * (moving[0] * moving[0] + moving[1] * moving[1] + moving[2] * moving[2]) / 3.0
    mask = lane_mask(lane[...])
    rows = [jnp.where(mask, living, 0.0).astype(FLOAT8)]
    rest = jnp.where(mask, 8.0 * energy, 0.0)
    for _ in range(3):
        piece = rest.astype(FLOAT8)
        rows.append(piece)
        rest = 16.0 * (rest - piece.astype(jnp.float32))
    weighted = jnp.concatenate(rows, 0)
    columns = sums.shape[1]
    place = face_column(column[...]) if faces else inner_column(column[...])
    term = lax.dot_general(
        weighted,
        column_hot(place, columns).astype(FLOAT8),
        (((1,), (1,)), ((), ())),
        preferred_element_type=jnp.float32,
    )
    sums[:NZ] += term[:NZ]
    small = term[2 * NZ : 3 * NZ] * (1 / 128) + term[3 * NZ :] * (1 / 2048)
    sums[NZ:] += term[NZ : 2 * NZ] * 0.125 + small

    @pl.when(pl.program_id(0) == pl.num_programs(0) - 1)
    def _():
        rows = columns // CX
        layers = NZ // (2 * HALO)
        for layer in range(0, CX, layers):
            part = pl.ds(layer * rows, layers * rows)
            span = pl.ds(layer, layers)
            load = (COUPLING * sums[:NZ, part].T).reshape(layers, rows, NZ)
            kinetic = (COUPLING * sums[NZ:, part].T).reshape(layers, rows, NZ)
            if faces:
                for target, side in ((first, slice(0, HALO)), (second, slice(HALO, 2 * HALO))):
                    target[span, :HALO] = load[:, side]
                    target[span, HALO:] = kinetic[:, side]
                for target, side in (
                    (sends[0], slice(0, NEAR)),
                    (sends[1], slice(2 * HALO - NEAR, 2 * HALO)),
                ):
                    pack(target, layer // 4, jnp.concatenate([load[:, side], kinetic[:, side]], 1))
            else:
                first[span] = load
                second[span] = kinetic


def pack(target, first, rows):
    fours = rows.reshape(rows.shape[0] // 4, 4, 2 * NEAR, NZ)
    span = pl.ds(first, fours.shape[0])
    for k in range(3):
        target[span, k] = jnp.concatenate([fours[:, k], fours[:, 3, 2 * k : 2 * k + 2]], 1)


def unpack(tiles):
    kept = [tiles[:, k] for k in range(3)]
    fourth = jnp.concatenate([tile[:, 2 * NEAR :] for tile in kept], 1)
    fours = jnp.stack([tile[:, : 2 * NEAR] for tile in kept] + [fourth], 1)
    return fours.reshape(4 * fours.shape[0], 2 * NEAR, NZ)


def blocks_of(shape, block):
    return pl.BlockSpec(shape + (block,), lambda i: (0,) * len(shape) + (i,))


def whole_of(*shape):
    return pl.BlockSpec(shape, lambda i: (0,) * len(shape))


def bin_atoms(faces, count, column, lane, velocities):
    slots = column.shape[1]
    block = min(BLOCK, slots)
    rows = 2 * HALO if faces else INNER
    result = (CX, rows, NZ)
    send = (CX // 4, 3, 2 * HALO, NZ)
    results = [result] * 2 + ([send] * 2 if faces else [])
    return pl.pallas_call(
        functools.partial(bin_kernel, block, faces),
        grid=(slots // block,),
        out_shape=[f32(*shape) for shape in results],
        in_specs=[SMEM, blocks_of((1,), block), blocks_of((1,), block), blocks_of((3, 1), block)],
        out_specs=[whole_of(*shape) for shape in results],
        scratch_shapes=[pltpu.VMEM((2 * NZ, CX * rows), jnp.float32)],
        compiler_params=params(63 if faces else 48),
        cost_estimate=pl.CostEstimate(
            flops=6 * slots * CX * rows * NZ, bytes_accessed=4_000_000, transcendentals=0
        ),
        name="bin_faces" if faces else "bin_inner",
    )(count, column, lane, velocities)


def read_kernel(block, count, te, column, lane, velocities, noise, forces, pair):
    @pl.when(pl.program_id(0) == 0)
    def _():
        rest = te[...].T * 8.0
        for k in range(3):
            piece = rest.astype(FLOAT8)
            pair[k * NZ : (k + 1) * NZ] = piece
            rest = (rest - piece.astype(jnp.float32)) * 16.0

    hot = column_hot(column[...], COLS).astype(FLOAT8)
    rows = jnp.dot(pair[...], hot, preferred_element_type=jnp.float32)
    value = rows[:NZ] * 0.125 + (rows[NZ : 2 * NZ] * (1 / 128) + rows[2 * NZ :] * (1 / 2048))
    picked = jnp.where(lane_mask(lane[...]), value, 0.0)
    te_atom = jnp.sum(picked, axis=0, keepdims=True)
    drive = jnp.sqrt(2.0 * FRICTION * te_atom)
    forces[...] = living_of(count, block) * (-FRICTION * velocities[...] + drive * noise[...])


def read_atoms(count, te, column, lane, velocities, noise):
    slots = column.shape[1]
    block = min(BLOCK, slots)
    return pl.pallas_call(
        functools.partial(read_kernel, block),
        grid=(slots // block,),
        out_shape=f32(3, 1, slots),
        in_specs=[
            SMEM,
            whole_of(COLS, NZ),
            blocks_of((1,), block),
            blocks_of((1,), block),
            blocks_of((3, 1), block),
            blocks_of((3, 1), block),
        ],
        out_specs=blocks_of((3, 1), block),
        scratch_shapes=[pltpu.VMEM((3 * NZ, COLS), FLOAT8)],
        compiler_params=params(48),
        cost_estimate=pl.CostEstimate(
            flops=4 * slots * COLS * NZ, bytes_accessed=4_000_000, transcendentals=0
        ),
        name="read_atoms",
    )(count, te, column, lane, velocities, noise)


def to_both_sides(head, tail, axis):
    count = lax.axis_size(axis)
    from_before = lax.ppermute(tail, axis, [(i, (i + 1) % count) for i in range(count)])
    from_after = lax.ppermute(head, axis, [((i + 1) % count, i) for i in range(count)])
    return from_before, from_after


def exchanged(blocks):
    return lax.all_to_all(blocks, "gy", split_axis=0, concat_axis=0, tiled=True)


def on_device(te_init, source, velocities, noise, cell_index, cell_lane, brick_atoms):
    parts = lax.axis_size("gy")
    layers = te_init.shape[0]
    fields = widened(te_init, source, parts)
    fields = exchanged(fields.reshape(2 * parts * layers, ROWS, NZ))

    column = cell_index[0]
    lane = cell_lane[0]
    moving = velocities[:, 0]
    own_head, own_tail, head, tail = bin_atoms(True, brick_atoms, column, lane, moving)
    before, after = to_both_sides(head, tail, "gy")
    load, kinetic = bin_atoms(False, brick_atoms, column, lane, moving)

    position = lax.axis_index("gx")
    final = lax.axis_size("gx") - 1
    place = jnp.stack([position == 0, position == final]).astype(jnp.int32)
    te, source = unmixed(parts, fields)
    head, tail, halo = edges(own_head, own_tail, load, kinetic, before, after, te, source)
    lo, hi = to_both_sides(head, tail, "gx")
    inner, heat, load = first_interior(own_head, own_tail, load, kinetic, halo, te, source)
    middle, head, tail = bands(False, place, te, heat, load, lo, hi, lo, hi, inner)

    before, after = to_both_sides(head, tail, "gy")
    te, head, tail = second_brick(middle, before, after)
    te_lo, te_hi = to_both_sides(head, tail, "gx")
    inner = second_interior(te, heat, load)
    (te,) = bands(True, place, te, heat, load, te_lo, te_hi, lo, hi, inner)

    electron = exchanged(te).reshape(parts, layers, CY, NZ).transpose(1, 0, 2, 3)
    electron = electron.reshape(layers, parts * CY, NZ)
    forces = read_atoms(brick_atoms, te.reshape(COLS, NZ), column, lane, moving, noise[:, 0])
    return (electron, forces[:, None])


def solution(mesh):
    return jax.shard_map(
        on_device,
        mesh=mesh,
        in_specs=(
            P(("gx", "gy"), None, None),
            P(("gx", "gy"), None, None),
            P(None, "gx", "gy", None),
            P(None, "gx", "gy", None),
            P("gx", "gy", None),
            P("gx", "gy", None),
            P("gx", "gy"),
        ),
        out_specs=(P(("gx", "gy"), None, None), P(None, "gx", "gy", None)),
        check_vma=False,
    )
```

```python
import functools

import jax
import jax.numpy as jnp
from jax import lax
from jax.experimental import pallas as pl
from jax.experimental.pallas import tpu as pltpu
from jax.sharding import PartitionSpec as P

CX = 48
CY = 32
NZ = 128
CONDUCTIVITY = 0.08
COUPLING = 0.1
FRICTION = 0.5

HALO = 4
NEAR = HALO - 1
ROWS = CY + 2 * HALO
COLS = CX * CY
BLOCK = 4096
FLOAT8 = jnp.float8_e4m3fn
MIB = 1024 * 1024

VMEM = pl.BlockSpec(memory_space=pltpu.VMEM)
SMEM = pl.BlockSpec(memory_space=pltpu.SMEM)
ANY = pl.BlockSpec(memory_space=pl.ANY)


def params(mib):
    return pltpu.CompilerParams(vmem_limit_bytes=mib * MIB)


def f32(*shape):
    return jax.ShapeDtypeStruct(shape, jnp.float32)


def inverse(value):
    return 1.0 / value


def flux(u, r, v, q):
    return (v - u) * inverse(r + q)


def renewed(u, c, r, below, above, heat, load):
    rows = u.shape[0]
    side = flux(u, r, pltpu.roll(u, rows - 1, 0), pltpu.roll(r, rows - 1, 0))
    lane = flux(u, r, pltpu.roll(u, NZ - 1, 1), pltpu.roll(r, NZ - 1, 1))
    total = (above - below) + (side - pltpu.roll(side, 1, 0)) + (lane - pltpu.roll(lane, 1, 1))
    return (u * c + (2.0 * CONDUCTIVITY) * total + heat) * inverse(c + load)


def with_root(u):
    c = 1.0 + u * u
    return c, lax.rsqrt(c)


def interior_steps(first, second, heat, load, out):
    def step(source, target, shift, spoiled, group):
        below_u = source[spoiled]
        _, below_r = with_root(below_u)
        u = source[spoiled + 1]
        c, r = with_root(u)

        def turn(i, carry):
            u, c, r, below = carry
            for g in range(group):
                layer = i * group + (spoiled + g)
                v = source[layer + 2]
                cv, rv = with_root(v)
                above = flux(u, r, v, rv)
                target[layer + shift] = renewed(u, c, r, below, above, heat[layer], load[layer])
                u, c, r, below = v, cv, rv, above
            return u, c, r, below

        turns = (CX - 2 * spoiled) // group
        lax.fori_loop(0, turns, turn, (u, c, r, flux(below_u, below_r, u, r)))

    for buffer in (first, second):
        buffer[0] = first[1]
        buffer[CX + 1] = first[CX]
    step(first, second, 1, 0, 8)
    step(second, first, 1, 0, 8)
    step(first, second, 1, NEAR, 7)
    step(second, out, 0, HALO, 8)


def padded_brick():
    return pltpu.VMEM((CX + 2, ROWS, NZ), jnp.float32)


def second_interior_kernel(te, heat, load, out, first, second):
    first[pl.ds(1, CX)] = te[...]
    interior_steps(first, second, heat, load, out)


def second_interior(te, heat, load):
    return pl.pallas_call(
        second_interior_kernel,
        out_shape=f32(CX, ROWS, NZ),
        in_specs=[VMEM] * 3,
        out_specs=VMEM,
        scratch_shapes=[padded_brick()] * 2,
        compiler_params=params(32),
        cost_estimate=pl.CostEstimate(flops=0, bytes_accessed=25_000_000, transcendentals=0),
        name="interior",
    )(te, heat, load)


def first_interior_kernel(
    parts, own_head, own_tail, load_in, kinetic, halo, fields, out, heat, load, *scratch
):
    first, second, source, sems = scratch
    layers = CX // parts
    fetches = []
    for j in range(parts):
        at = 2 * j * layers
        te_here = first.at[pl.ds(1 + j * layers, layers)]
        source_here = source.at[pl.ds(j * layers, layers)]
        for k, here in enumerate((te_here, source_here)):
            there = fields.at[pl.ds(at + k * layers, layers)]
            fetches.append(pltpu.make_async_copy(there, here, sems.at[2 * j + k]))
    for fetch in fetches:
        fetch.start()
    for i in range(parts):
        span = pl.ds(i * layers, layers)
        load[span] = side_by_side(own_head, load_in, own_tail, halo, span, 0)
    for fetch in fetches:
        fetch.wait()
    for i in range(parts):
        span = pl.ds(i * layers, layers)
        heat[span] = source[span] + side_by_side(
            own_head, kinetic, own_tail, halo, span, 1
        )
    interior_steps(first, second, heat, load, out)


def side_by_side(own_head, inner, own_tail, halo, span, field):
    rows = slice(field * HALO, field * HALO + HALO)
    return jnp.concatenate(
        [own_head[span, rows], inner[span], own_tail[span, rows], halo[field, span]], 1
    )


def first_interior(parts, *arrays):
    whole = f32(CX, ROWS, NZ)
    return pl.pallas_call(
        functools.partial(first_interior_kernel, parts),
        out_shape=[whole] * 3,
        in_specs=[VMEM] * 5 + [ANY],
        out_specs=[VMEM] * 3,
        scratch_shapes=[padded_brick()] * 2
        + [pltpu.VMEM((CX, ROWS, NZ), jnp.float32)]
        + [pltpu.SemaphoreType.DMA((2 * parts,))],
        compiler_params=params(32),
        cost_estimate=pl.CostEstimate(flops=0, bytes_accessed=30_000_000, transcendentals=0),
        name="first_interior",
    )(*arrays)


def band_steps(us, heats, loads, closed_face, closed):
    for step in range(1, HALO + 1):
        us = list(us)
        roots = [with_root(u) for u in us]
        faces = []
        for i in range(len(us) - 1):
            face = flux(us[i], roots[i][1], us[i + 1], roots[i + 1][1])
            if i + step - 1 == closed_face:
                face = jnp.where(closed, 0.0, face)
            faces.append(face)
        us = [
            renewed(
                us[i],
                *roots[i],
                faces[i - 1],
                faces[i],
                heats[i + step - 2],
                loads[i + step - 2],
            )
            for i in range(1, len(us) - 1)
        ]
    return us


def bands_kernel(last, place, te, heat, load, te_lo, te_hi, lo, hi, inner, out, *faces):
    many = 2 * HALO
    near = HALO + NEAR
    low = band_steps(
        [te_lo[i] for i in range(HALO)] + [te[i] for i in range(many)],
        [lo[HALO + i] for i in range(NEAR)] + [heat[i] for i in range(near)],
        [lo[HALO + NEAR + i] for i in range(NEAR)] + [load[i] for i in range(near)],
        HALO - 1,
        place[0] == 1,
    )
    high = band_steps(
        [te[te.shape[0] - many + i] for i in range(many)] + [te_hi[i] for i in range(HALO)],
        [heat[CX - near + i] for i in range(near)] + [hi[HALO + i] for i in range(NEAR)],
        [load[CX - near + i] for i in range(near)] + [hi[HALO + NEAR + i] for i in range(NEAR)],
        many - 1,
        place[1] == 1,
    )
    out[pl.ds(HALO, CX - many)] = inner[pl.ds(HALO, CX - many), :CY]
    for i in range(HALO):
        out[i] = low[i][:CY]
        out[CX - HALO + i] = high[i][:CY]
    if not last:
        head, tail = faces
        half = CX // 2
        head[:, :HALO] = out[:half, :HALO]
        head[:, HALO:] = out[half:, :HALO]
        tail[:, :HALO] = out[:half, CY - HALO :]
        tail[:, HALO:] = out[half:, CY - HALO :]


def bands(last, place, te, heat, load, te_lo, te_hi, lo, hi, inner):
    face = f32(CX // 2, 2 * HALO, NZ)
    shapes = [f32(CX, CY, NZ)] + ([] if last else [face, face])
    return pl.pallas_call(
        functools.partial(bands_kernel, last),
        out_shape=shapes,
        in_specs=[SMEM] + [VMEM] * 8,
        out_specs=[VMEM] * len(shapes),
        compiler_params=params(32),
        cost_estimate=pl.CostEstimate(flops=0, bytes_accessed=8_000_000, transcendentals=0),
        name="bands",
    )(place, te, heat, load, te_lo, te_hi, lo, hi, inner)


def edges_kernel(parts, *refs):
    inside, (fields, ends, head, tail, halo, here, source, sems) = refs[:6], refs[6:]
    own_head, own_tail, load_in, kinetic, before, after = inside
    layers = CX // parts
    many = 2 * HALO
    fetches = []

    def fetch(there, here):
        copy = pltpu.make_async_copy(there, here, sems.at[len(fetches)])
        copy.start()
        fetches.append(copy)

    for k, first in enumerate((0, CX - many)):
        layer = first
        while layer < first + many:
            part = layer // layers
            count = min(first + many, (part + 1) * layers) - layer
            there = fields.at[pl.ds(layer + part * layers, count)]
            fetch(there, here.at[pl.ds(k * many + layer - first, count)])
            layer += count
    for k, first in enumerate((0, CX - NEAR)):
        layer = first
        while layer < first + NEAR:
            part = layer // layers
            count = min(first + NEAR, (part + 1) * layers) - layer
            there = fields.at[pl.ds(layer + (part + 1) * layers, count)]
            fetch(there, source.at[k, pl.ds(layer - first, count)])
            layer += count
    before, after = unpack(before), unpack(after)
    gap = jnp.zeros((CX, 2 * HALO - 2 * NEAR, NZ), jnp.float32)
    for field in range(2):
        rows = slice(field * NEAR, field * NEAR + NEAR)
        halo[field] = jnp.concatenate([after[:, rows], gap, before[:, rows]], 1)
    for copy in fetches:
        copy.wait()
    ends[...] = here[...]
    for k, (target, at) in enumerate(((head, 0), (tail, 2 * many - HALO))):
        span = pl.ds((0, CX - NEAR)[k], NEAR)
        target[:HALO] = here[pl.ds(at, HALO)]
        target[pl.ds(HALO, NEAR)] = source[k] + side_by_side(
            own_head, kinetic, own_tail, halo, span, 1
        )
        target[pl.ds(HALO + NEAR, NEAR)] = side_by_side(
            own_head, load_in, own_tail, halo, span, 0
        )


def edges(parts, *arrays):
    edge = f32(HALO + 2 * NEAR, ROWS, NZ)
    ends = (4 * HALO, ROWS, NZ)
    return pl.pallas_call(
        functools.partial(edges_kernel, parts),
        out_shape=[f32(*ends), edge, edge, f32(2, CX, 2 * HALO, NZ)],
        in_specs=[VMEM] * 6 + [ANY],
        out_specs=[VMEM] * 4,
        scratch_shapes=[
            pltpu.VMEM(ends, jnp.float32),
            pltpu.VMEM((2, NEAR, ROWS, NZ), jnp.float32),
            pltpu.SemaphoreType.DMA((16,)),
        ],
        compiler_params=params(32),
        cost_estimate=pl.CostEstimate(flops=0, bytes_accessed=2_000_000, transcendentals=0),
        name="edges",
    )(*arrays)


def widen_kernel(parts, te, source, out, here, halo, in_sems, out_sems):
    layers = te.shape[0]
    fetches = [
        pltpu.make_async_copy(field, here.at[f], in_sems.at[f])
        for f, field in enumerate((te, source))
    ]
    for fetch in fetches:
        fetch.start()
    sends = []
    for f in range(2):
        fetches[f].wait()
        span = pl.ds(f * layers, layers)
        for j in range(parts):
            after = (j + 1) % parts * CY
            before = (j - 1) % parts * CY + CY - HALO
            halo[j, span] = jnp.concatenate(
                [here[f, :, pl.ds(after, HALO)], here[f, :, pl.ds(before, HALO)]], 1
            )
            own = here.at[f, :, pl.ds(j * CY, CY)]
            for k, (piece, rows) in enumerate(
                ((own, pl.ds(0, CY)), (halo.at[j, span], pl.ds(CY, 2 * HALO)))
            ):
                send = pltpu.make_async_copy(piece, out.at[j, span, rows], out_sems.at[f, j, k])
                send.start()
                sends.append(send)
    for send in sends:
        send.wait()


def widened(te, source, parts):
    layers = te.shape[0]
    return pl.pallas_call(
        functools.partial(widen_kernel, parts),
        out_shape=f32(parts, 2 * layers, ROWS, NZ),
        in_specs=[ANY] * 2,
        out_specs=ANY,
        scratch_shapes=[
            pltpu.VMEM((2,) + te.shape, jnp.float32),
            pltpu.VMEM((parts, 2 * layers, 2 * HALO, NZ), jnp.float32),
            pltpu.SemaphoreType.DMA((2,)),
            pltpu.SemaphoreType.DMA((2, parts, 2)),
        ],
        compiler_params=params(63),
        cost_estimate=pl.CostEstimate(flops=0, bytes_accessed=4_000_000, transcendentals=0),
        name="widen",
    )(te, source)


def second_kernel(middle, before, after, te, head, tail):
    half = CX // 2
    te[:, :CY] = middle[...]
    te[:half, CY:] = jnp.concatenate([after[:, :HALO], before[:, :HALO]], 1)
    te[half:, CY:] = jnp.concatenate([after[:, HALO:], before[:, HALO:]], 1)
    head[...] = te[:HALO]
    tail[...] = te[CX - HALO :]


def second_brick(middle, before, after):
    edge = f32(HALO, ROWS, NZ)
    return pl.pallas_call(
        second_kernel,
        out_shape=[f32(CX, ROWS, NZ), edge, edge],
        in_specs=[VMEM] * 3,
        out_specs=[VMEM] * 3,
        compiler_params=params(32),
        cost_estimate=pl.CostEstimate(flops=0, bytes_accessed=4_000_000, transcendentals=0),
        name="second_brick",
    )(middle, before, after)


INNER = CY - 2 * HALO


def column_hot(column, columns):
    ids = lax.broadcasted_iota(jnp.int16, (columns, column.shape[1]), 0)
    hot = ids == column.astype(jnp.int16)
    return jnp.where(hot, jnp.bfloat16(1), jnp.bfloat16(0))


def face_column(column):
    layer, row = column // CY, column % CY
    side = jnp.where(row < HALO, row, jnp.where(row >= CY - HALO, row - INNER, -1))
    return jnp.where(side < 0, -1, layer * 2 * HALO + side)


def inner_column(column):
    layer, row = column // CY, column % CY
    inside = (row >= HALO) & (row < CY - HALO)
    return jnp.where(inside, layer * INNER + row - HALO, -1)


def lane_mask(lane):
    return lax.broadcasted_iota(jnp.int32, (NZ, lane.shape[1]), 0) == lane


def living_of(count, block):
    slot = pl.program_id(0) * block + lax.broadcasted_iota(jnp.int32, (1, block), 1)
    return jnp.where(slot < count[0, 0], 1.0, 0.0)


def bin_kernel(block, faces, count, column, lane, velocities, first, second, *rest):
    *sends, sums = rest

    @pl.when(pl.program_id(0) == 0)
    def _():
        sums[...] = jnp.zeros_like(sums)

    living = living_of(count, block)
    moving = velocities[...]
    energy = living * (moving[0] * moving[0] + moving[1] * moving[1] + moving[2] * moving[2]) / 3.0
    mask = lane_mask(lane[...])
    rows = [jnp.where(mask, living, 0.0).astype(FLOAT8)]
    rest = jnp.where(mask, 8.0 * energy, 0.0)
    for _ in range(3):
        piece = rest.astype(FLOAT8)
        rows.append(piece)
        rest = 16.0 * (rest - piece.astype(jnp.float32))
    weighted = jnp.concatenate(rows, 0)
    columns = sums.shape[1]
    place = face_column(column[...]) if faces else inner_column(column[...])
    term = lax.dot_general(
        weighted,
        column_hot(place, columns).astype(FLOAT8),
        (((1,), (1,)), ((), ())),
        preferred_element_type=jnp.float32,
    )
    sums[:NZ] += term[:NZ]
    small = term[2 * NZ : 3 * NZ] * (1 / 128) + term[3 * NZ :] * (1 / 2048)
    sums[NZ:] += term[NZ : 2 * NZ] * 0.125 + small

    @pl.when(pl.program_id(0) == pl.num_programs(0) - 1)
    def _():
        rows = columns // CX
        layers = NZ // (2 * HALO)
        for layer in range(0, CX, layers):
            part = pl.ds(layer * rows, layers * rows)
            span = pl.ds(layer, layers)
            load = (COUPLING * sums[:NZ, part].T).reshape(layers, rows, NZ)
            kinetic = (COUPLING * sums[NZ:, part].T).reshape(layers, rows, NZ)
            if faces:
                for target, side in ((first, slice(0, HALO)), (second, slice(HALO, 2 * HALO))):
                    target[span, :HALO] = load[:, side]
                    target[span, HALO:] = kinetic[:, side]
                for target, side in (
                    (sends[0], slice(0, NEAR)),
                    (sends[1], slice(2 * HALO - NEAR, 2 * HALO)),
                ):
                    pack(target, layer // 4, jnp.concatenate([load[:, side], kinetic[:, side]], 1))
            else:
                first[span] = load
                second[span] = kinetic


def pack(target, first, rows):
    fours = rows.reshape(rows.shape[0] // 4, 4, 2 * NEAR, NZ)
    span = pl.ds(first, fours.shape[0])
    for k in range(3):
        target[span, k] = jnp.concatenate([fours[:, k], fours[:, 3, 2 * k : 2 * k + 2]], 1)


def unpack(tiles):
    kept = [tiles[:, k] for k in range(3)]
    fourth = jnp.concatenate([tile[:, 2 * NEAR :] for tile in kept], 1)
    fours = jnp.stack([tile[:, : 2 * NEAR] for tile in kept] + [fourth], 1)
    return fours.reshape(4 * fours.shape[0], 2 * NEAR, NZ)


def blocks_of(shape, block):
    return pl.BlockSpec(shape + (block,), lambda i: (0,) * len(shape) + (i,))


def whole_of(*shape):
    return pl.BlockSpec(shape, lambda i: (0,) * len(shape))


def bin_atoms(faces, count, column, lane, velocities):
    slots = column.shape[1]
    block = min(BLOCK, slots)
    rows = 2 * HALO if faces else INNER
    result = (CX, rows, NZ)
    send = (CX // 4, 3, 2 * HALO, NZ)
    results = [result] * 2 + ([send] * 2 if faces else [])
    return pl.pallas_call(
        functools.partial(bin_kernel, block, faces),
        grid=(slots // block,),
        out_shape=[f32(*shape) for shape in results],
        in_specs=[SMEM, blocks_of((1,), block), blocks_of((1,), block), blocks_of((3, 1), block)],
        out_specs=[whole_of(*shape) for shape in results],
        scratch_shapes=[pltpu.VMEM((2 * NZ, CX * rows), jnp.float32)],
        compiler_params=params(63 if faces else 48),
        cost_estimate=pl.CostEstimate(
            flops=6 * slots * CX * rows * NZ, bytes_accessed=4_000_000, transcendentals=0
        ),
        name="bin_faces" if faces else "bin_inner",
    )(count, column, lane, velocities)


def read_kernel(block, count, te, column, lane, velocities, noise, forces, pair):
    @pl.when(pl.program_id(0) == 0)
    def _():
        rest = te[...].T * 8.0
        for k in range(3):
            piece = rest.astype(FLOAT8)
            pair[k * NZ : (k + 1) * NZ] = piece
            rest = (rest - piece.astype(jnp.float32)) * 16.0

    hot = column_hot(column[...], COLS).astype(FLOAT8)
    rows = jnp.dot(pair[...], hot, preferred_element_type=jnp.float32)
    value = rows[:NZ] * 0.125 + (rows[NZ : 2 * NZ] * (1 / 128) + rows[2 * NZ :] * (1 / 2048))
    picked = jnp.where(lane_mask(lane[...]), value, 0.0)
    te_atom = jnp.sum(picked, axis=0, keepdims=True)
    drive = jnp.sqrt(2.0 * FRICTION * te_atom)
    forces[...] = living_of(count, block) * (-FRICTION * velocities[...] + drive * noise[...])


def read_atoms(count, te, column, lane, velocities, noise):
    slots = column.shape[1]
    block = min(2 * BLOCK, slots)
    return pl.pallas_call(
        functools.partial(read_kernel, block),
        grid=(slots // block,),
        out_shape=f32(3, 1, slots),
        in_specs=[
            SMEM,
            whole_of(COLS, NZ),
            blocks_of((1,), block),
            blocks_of((1,), block),
            blocks_of((3, 1), block),
            blocks_of((3, 1), block),
        ],
        out_specs=blocks_of((3, 1), block),
        scratch_shapes=[pltpu.VMEM((3 * NZ, COLS), FLOAT8)],
        compiler_params=params(60),
        cost_estimate=pl.CostEstimate(
            flops=4 * slots * COLS * NZ, bytes_accessed=4_000_000, transcendentals=0
        ),
        name="read_atoms",
    )(count, te, column, lane, velocities, noise)


def to_both_sides(head, tail, axis):
    count = lax.axis_size(axis)
    from_before = lax.ppermute(tail, axis, [(i, (i + 1) % count) for i in range(count)])
    from_after = lax.ppermute(head, axis, [((i + 1) % count, i) for i in range(count)])
    return from_before, from_after


def exchanged(blocks):
    return lax.all_to_all(blocks, "gy", split_axis=0, concat_axis=0, tiled=True)


def on_device(te_init, source, velocities, noise, cell_index, cell_lane, brick_atoms):
    parts = lax.axis_size("gy")
    layers = te_init.shape[0]
    fields = widened(te_init, source, parts)
    fields = exchanged(fields.reshape(2 * parts * layers, ROWS, NZ))

    column = cell_index[0]
    lane = cell_lane[0]
    moving = velocities[:, 0]
    own_head, own_tail, head, tail = bin_atoms(True, brick_atoms, column, lane, moving)
    before, after = to_both_sides(head, tail, "gy")
    load, kinetic = bin_atoms(False, brick_atoms, column, lane, moving)

    position = lax.axis_index("gx")
    final = lax.axis_size("gx") - 1
    place = jnp.stack([position == 0, position == final]).astype(jnp.int32)
    ends, head, tail, halo = edges(
        parts, own_head, own_tail, load, kinetic, before, after, fields
    )
    lo, hi = to_both_sides(head, tail, "gx")
    inner, heat, load = first_interior(parts, own_head, own_tail, load, kinetic, halo, fields)
    middle, head, tail = bands(False, place, ends, heat, load, lo, hi, lo, hi, inner)

    before, after = to_both_sides(head, tail, "gy")
    te, head, tail = second_brick(middle, before, after)
    te_lo, te_hi = to_both_sides(head, tail, "gx")
    inner = second_interior(te, heat, load)
    (te,) = bands(True, place, te, heat, load, te_lo, te_hi, lo, hi, inner)

    electron = exchanged(te).reshape(parts, layers, CY, NZ).transpose(1, 0, 2, 3)
    electron = electron.reshape(layers, parts * CY, NZ)
    forces = read_atoms(brick_atoms, te.reshape(COLS, NZ), column, lane, moving, noise[:, 0])
    return (electron, forces[:, None])


def solution(mesh):
    return jax.shard_map(
        on_device,
        mesh=mesh,
        in_specs=(
            P(("gx", "gy"), None, None),
            P(("gx", "gy"), None, None),
            P(None, "gx", "gy", None),
            P(None, "gx", "gy", None),
            P("gx", "gy", None),
            P("gx", "gy", None),
            P("gx", "gy"),
        ),
        out_specs=(P(("gx", "gy"), None, None), P(None, "gx", "gy", None)),
        check_vma=False,
    )
```
